32 devices in a mesh: pipe: 4 (over y, core), fsdp: 4 (over z), tensor: 2 (over x).
Axes of the slice: x: 2, y: 2, z: 4, core: 2. Of those that a mesh axis runs over, the one named last changes fastest.
Arguments:
- tokens: bfloat16 [768, 4096], P('fsdp', 'tensor'), may hold values from -8 to 8
- norm_gains: float32 [4, 4096], P('pipe'), may hold values from 0.1 to 1.9
- q_blocks: bfloat16 [4, 4, 16, 256, 256], P('pipe', None, 'tensor', 'fsdp'), may hold values from -1 to 1
- k_blocks: bfloat16 [4, 4, 16, 256, 256], P('pipe', None, 'tensor', 'fsdp'), may hold values from -1 to 1
- v_blocks: bfloat16 [4, 4, 16, 256, 256], P('pipe', None, 'tensor', 'fsdp'), may hold values from -0.1875 to 0.1875
- o_blocks: bfloat16 [4, 4, 16, 256, 256], P('pipe', 'tensor', None, 'fsdp'), may hold values from -0.1875 to 0.1875
- q_rows: int32 [4, 4, 16], P('pipe', None, 'tensor'), may hold values from 0 to 15, as said below
- k_rows: int32 [4, 4, 16], P('pipe', None, 'tensor'), may hold values from 0 to 15, as said below
- v_rows: int32 [4, 4, 16], P('pipe', None, 'tensor'), may hold values from 0 to 15, as said below
- o_rows: int32 [4, 4, 16], P('pipe', 'tensor'), may hold values from 0 to 7, as said below
- mask_blocks: int32 [12, 4, 4], P('fsdp'), may hold values from 0 to 1, as said below
Outputs:
- activations: bfloat16 [4, 768, 4096], P('pipe', 'fsdp', 'tensor')
The draws below stay inside these ranges and needn't reach their ends.
Inputs may be any that keep to these rules, and one draw needn't show every extreme that they name: `q_rows`: for each section and column block the 4 listed input blocks are distinct. `k_rows`: for each section and column block the 4 listed input blocks are distinct. `v_rows`: for each section and column block the 4 listed input blocks are distinct. `o_rows`: entries k and k2 with k // 2 == k2 // 2 name distinct head blocks of one column block. Every diagonal block mask_blocks[n, i, i] is 1.
All inputs are finite; a program needn't handle non-finite values.
Results may differ from the reference program's by a relative error of at most 0.017.
Values may be sent and summed in bfloat16 or wider, within the bound.
No kernel may reach another device: no remote copies, remote signals or barrier semaphores. Data moves between devices by JAX's collectives and lax.ppermute only.
A program may use at most 64 MiB of HBM per device.

```python
import jax
import jax.numpy as jnp
from jax import lax

D = 4096
HEADS = 32
HD = 128
BS = 256
L = 64
MBLK = 16
SECTIONS = 4
TOKENS = 768
SEQS = 12
LB = 4
KB = 16
PER = 4
HB = 16
HB_DEV = 8
OPER_T = 2
OPER = 4


def pick_distinct(base_key, groups, total, wanted):
    key_list = jax.random.split(base_key, groups)
    perm_rows = jax.vmap(lambda single: jax.random.permutation(single, total))(key_list)
    return perm_rows[:, :wanted]


def input_pattern(key, salt):
    chosen = pick_distinct(jax.random.fold_in(key, salt), SECTIONS * HB, KB, PER)
    return jnp.transpose(chosen.reshape(SECTIONS, HB, PER), (0, 2, 1)).astype(jnp.int32)


def draw_q_rows(key, part):
    return input_pattern(key, 11)


def draw_k_rows(key, part):
    return input_pattern(key, 12)


def draw_v_rows(key, part):
    return input_pattern(key, 13)


def draw_o_rows(key, part):
    halves = OPER // OPER_T
    chosen = pick_distinct(jax.random.fold_in(key, 14), SECTIONS * halves * KB, HB_DEV, OPER_T)
    shaped = chosen.reshape(SECTIONS, halves, KB, OPER_T)
    return jnp.transpose(shaped, (0, 1, 3, 2)).reshape(SECTIONS, OPER, KB).astype(jnp.int32)


def draw_mask_blocks(key, part):
    random_bits = jax.random.randint(jax.random.fold_in(key, 15), (SEQS, LB, LB), 0, 2)
    diagonal = (jnp.arange(LB)[:, None] == jnp.arange(LB)[None, :]).astype(jnp.int32)
    return jnp.maximum(random_bits, diagonal[None]).astype(jnp.int32)


def project_weights(key, salt):
    base_key = jax.random.fold_in(key, salt)
    shape = (SECTIONS, PER, HB, BS, BS)
    spread = (PER * BS) ** (-0.5)
    values = jnp.clip(jax.random.normal(base_key, shape, jnp.float32), -6.0, 6.0) * spread
    return values.astype(jnp.bfloat16)


def draw_q_blocks(key, part):
    return project_weights(key, 41)


def draw_k_blocks(key, part):
    return project_weights(key, 42)


def draw_tokens(key, part):
    base_key = jax.random.fold_in(key, 31)
    values = jnp.clip(jax.random.normal(base_key, (TOKENS, D), jnp.float32), -6.0, 6.0)
    return values.astype(jnp.bfloat16)


def levels(stream_key, dims, pieces, smallest, high):
    def one(dim, parts):
        draws = jax.random.uniform(jax.random.fold_in(jax.random.fold_in(stream_key, 6), dim), (parts,), jnp.float32, smallest / len(pieces), high / len(pieces))
        return jnp.repeat(jnp.exp(draws), dims[dim] // parts).reshape((-1,) + (1,) * (len(dims) - dim - 1))

    gain = one(*pieces[0])
    for cut in pieces[1:]:
        gain = gain * one(*cut)
    return gain


def normal_values(own_key, extent, scale, limit, cuts=(), kind=jnp.bfloat16):
    values = jax.random.normal(own_key, extent, jnp.float32) * scale
    if len(cuts) > 0:
        values = levels(own_key, extent, cuts, -0.22, 0.18) * values
    return jnp.clip(values, min=-limit, max=limit).astype(kind)


def setup_inputs(seed: int = 0) -> dict:
    streams_of = jax.random.split(jax.random.key(seed), 12)
    tokens = draw_tokens(jax.random.fold_in(streams_of[11], 71), 0)
    norm_gains = jnp.clip(1.0 + 0.18 * jax.random.normal(streams_of[1], (SECTIONS, D), jnp.float32), 0.1, 1.9)
    q_blocks = draw_q_blocks(jax.random.fold_in(streams_of[11], 71), 0)
    k_blocks = draw_k_blocks(jax.random.fold_in(streams_of[11], 71), 0)
    v_blocks = normal_values(streams_of[4], (SECTIONS, PER, HB, BS, BS), (PER * BS) ** -0.5, 0.1875, ((0, 4), (2, 2), (3, 4)))
    o_blocks = normal_values(streams_of[5], (SECTIONS, OPER, KB, BS, BS), (OPER * BS) ** -0.5, 0.1875, ((0, 4), (1, 2), (3, 4)))
    q_rows = draw_q_rows(jax.random.fold_in(streams_of[11], 71), 0)
    k_rows = draw_k_rows(jax.random.fold_in(streams_of[11], 71), 0)
    v_rows = draw_v_rows(jax.random.fold_in(streams_of[11], 71), 0)
    o_rows = draw_o_rows(jax.random.fold_in(streams_of[11], 71), 0)
    mask_blocks = draw_mask_blocks(jax.random.fold_in(streams_of[11], 71), 0)
    return dict(tokens=tokens, norm_gains=norm_gains, q_blocks=q_blocks, k_blocks=k_blocks, v_blocks=v_blocks, o_blocks=o_blocks, q_rows=q_rows, k_rows=k_rows, v_rows=v_rows, o_rows=o_rows, mask_blocks=mask_blocks)


def rms_rows(in_rows, gain_row):
    values = in_rows.astype(jnp.float32)
    inv_rms = lax.rsqrt(lax.optimization_barrier(jnp.mean(values * values, axis=-1, keepdims=True)) + 1e-05)
    return (values * inv_rms * gain_row.astype(jnp.float32)).astype(jnp.bfloat16)

def block_project(in_rows, blocks, pattern):
    row_count = in_rows.shape[0]
    block_width = blocks.shape[-1]
    row_blocks = in_rows.reshape(row_count, -1, block_width)
    picked = row_blocks[:, pattern]
    product = jnp.einsum('rpcb,pcbe->rce', picked.astype(jnp.float32), blocks.astype(jnp.float32))
    return product.reshape(row_count, -1)

def attend(queries, keys_proj, values_proj, mask_now):
    seq_count = mask_now.shape[0]
    head_shape = (seq_count, L, HEADS, HD)
    scores = jnp.einsum('sqhd,skhd->shqk', queries.reshape(head_shape).astype(jnp.float32), keys_proj.reshape(head_shape).astype(jnp.float32)) * HD ** (-0.5)
    allowed = jnp.repeat(jnp.repeat(mask_now, MBLK, axis=1), MBLK, axis=2) == 1
    scores = jnp.where(allowed[:, None], scores, jnp.float32(-1e+30))
    row_max = lax.optimization_barrier(jnp.max(scores, axis=-1, keepdims=True))
    exp_scores = jnp.exp(scores - row_max)
    probs = (exp_scores / lax.optimization_barrier(jnp.sum(exp_scores, axis=-1, keepdims=True))).astype(jnp.bfloat16)
    attended = jnp.einsum('shqk,skhd->sqhd', probs.astype(jnp.float32), values_proj.reshape(head_shape).astype(jnp.float32))
    return attended.astype(jnp.bfloat16).reshape(seq_count * L, HEADS * HD)

def reference(tokens, norm_gains, q_blocks, k_blocks, v_blocks, o_blocks, q_rows, k_rows, v_rows, o_rows, mask_blocks):
    current = tokens
    outputs = []
    tensor_group = jnp.arange(OPER, dtype=jnp.int32) // OPER_T
    for section in range(SECTIONS):
        normed = rms_rows(current, norm_gains[section])
        queries = block_project(normed, q_blocks[section], q_rows[section]).astype(jnp.bfloat16)
        keys_proj = block_project(normed, k_blocks[section], k_rows[section]).astype(jnp.bfloat16)
        values_proj = block_project(normed, v_blocks[section], v_rows[section]).astype(jnp.bfloat16)
        attended = attend(queries, keys_proj, values_proj, mask_blocks)
        full_rows = (o_rows[section] + tensor_group[:, None] * HB_DEV).astype(jnp.int32)
        branch = block_project(attended, o_blocks[section], full_rows)
        current = (current.astype(jnp.float32) + branch).astype(jnp.bfloat16)
        outputs.append(current)
    return jnp.stack(outputs)
```

```python
import functools

import jax
import jax.numpy as jnp
from jax import lax
from jax.experimental import pallas as pl
from jax.experimental.pallas import tpu as pltpu
from jax.sharding import PartitionSpec as P

HD = 128
MBLK = 16
AXES = ("pipe", "fsdp", "tensor")
VMEM_LIMIT = 24 * 1024 * 1024


def hop(value, sizes, target):
    pipe, fsdp, tensor = sizes
    pairs = []
    for p in range(pipe):
        for z in range(fsdp):
            for x in range(tensor):
                to = target(p, z, x)
                if to is not None:
                    pairs.append(((p * fsdp + z) * tensor + x, (to[0] * fsdp + to[1]) * tensor + to[2]))
    return lax.ppermute(value, AXES, pairs)


def after(value, *earlier):
    return lax.optimization_barrier((value, *earlier))[0]


def gather_weights(parts, total, sems, pos_ref):
    copies = []
    for i, part in enumerate(parts):
        rows = part.shape[1]
        start = pl.multiple_of(pos_ref[i] * rows, rows)
        copy = pltpu.make_async_copy(part, total.at[:, pl.ds(start, rows), :], sems.at[i])
        copy.start()
        copies.append(copy)
    return copies


def attend_kernel(n_parts, slot_ref, pos_ref, near_ref, far_ref, gain_ref, allow_ref, *rest):
    parts = rest[:n_parts]
    out_ref, weights, normed, proj, sems = rest[n_parts:]
    copies = gather_weights(parts, weights, sems, pos_ref)
    half = near_ref.shape[0]
    rows = near_ref.shape[1]
    width = near_ref.shape[2]
    square = jnp.zeros((rows, width), jnp.float32)
    for t in range(2 * half):
        block = (near_ref if t < half else far_ref)[t % half].astype(jnp.float32)
        square += block * block
    mean = jnp.sum(square, axis=-1, keepdims=True) / (2 * half * width)
    inv_rms = lax.rsqrt(mean + 1e-05)
    for t in range(2 * half):
        block = (near_ref if t < half else far_ref)[t % half].astype(jnp.float32)
        normed[t] = (block * inv_rms * gain_ref[t]).astype(jnp.bfloat16)
    for copy in copies:
        copy.wait()
    cols = out_ref.shape[0]
    per = weights.shape[0] // (3 * cols)
    for kind in range(3):
        for c in range(cols):
            total = None
            for i in range(per):
                n = (kind * per + i) * cols + c
                term = jnp.dot(normed[slot_ref[n]], weights[n], preferred_element_type=jnp.float32)
                total = term if total is None else total + term
            proj[kind, c] = total.astype(jnp.bfloat16)
    seq_len = allow_ref.shape[1]
    for n in range(allow_ref.shape[0]):
        allowed = allow_ref[n] > 0
        span = pl.ds(n * seq_len, seq_len)
        for c in range(cols):
            for h in range(width // HD):
                lanes = pl.ds(h * HD, HD)
                scores = lax.dot_general(
                    proj[0, c, span, lanes],
                    proj[1, c, span, lanes],
                    (((1,), (1,)), ((), ())),
                    preferred_element_type=jnp.float32,
                ) * HD ** (-0.5)
                scores = jnp.where(allowed, scores, jnp.float32(-1e30))
                exp_scores = jnp.exp(scores - jnp.max(scores, axis=-1, keepdims=True))
                probs = exp_scores / jnp.sum(exp_scores, axis=-1, keepdims=True)
                attended = jnp.dot(
                    probs.astype(jnp.bfloat16), proj[2, c, span, lanes], preferred_element_type=jnp.float32
                )
                out_ref[c, span, lanes] = attended.astype(jnp.bfloat16)


def output_kernel(n_parts, slot_ref, pos_ref, near_ref, far_ref, u_ref, *rest):
    parts = rest[:n_parts]
    out_ref, weights, heads, sems, head_sems = rest[n_parts:]
    half = near_ref.shape[0]
    copies = gather_weights(parts, weights, sems, pos_ref)
    for i, ref in enumerate((near_ref, far_ref)):
        copy = pltpu.make_async_copy(ref, heads.at[pl.ds(i * half, half)], head_sems.at[i])
        copy.start()
        copies.append(copy)
    for copy in copies:
        copy.wait()
    cols = out_ref.shape[0]
    per = weights.shape[0] // cols
    for c in range(cols):
        total = None
        for i in range(per):
            n = i * cols + c
            term = jnp.dot(heads[slot_ref[n]], weights[n], preferred_element_type=jnp.float32)
            total = term if total is None else total + term
        out_ref[c] = (u_ref[c].astype(jnp.float32) + total).astype(jnp.bfloat16)


SMEM = pl.BlockSpec(memory_space=pltpu.SMEM)
VMEM = pl.BlockSpec(memory_space=pltpu.VMEM)
ANY = pl.BlockSpec(memory_space=pl.ANY)


def attend(slots, pos, near, far, gain, allow, parts):
    half, rows, width = near.shape
    cols = 2
    count = parts[0].shape[0]
    depth = sum(part.shape[1] for part in parts)
    return pl.pallas_call(
        functools.partial(attend_kernel, len(parts)),
        out_shape=jax.ShapeDtypeStruct((cols, rows, width), jnp.bfloat16),
        in_specs=[SMEM, SMEM, VMEM, VMEM, VMEM, VMEM] + [ANY] * len(parts),
        out_specs=VMEM,
        scratch_shapes=[
            pltpu.VMEM((count, depth, width), jnp.bfloat16),
            pltpu.VMEM((2 * half, rows, width), jnp.bfloat16),
            pltpu.VMEM((3, cols, rows, width), jnp.bfloat16),
            pltpu.SemaphoreType.DMA((len(parts),)),
        ],
        compiler_params=pltpu.CompilerParams(vmem_limit_bytes=VMEM_LIMIT),
        name="attend",
    )(slots, pos, near, far, gain, allow, *parts)


def project_out(slots, pos, near, far, u_piece, parts):
    half, rows, width = near.shape
    count = parts[0].shape[0]
    depth = sum(part.shape[1] for part in parts)
    return pl.pallas_call(
        functools.partial(output_kernel, len(parts)),
        out_shape=jax.ShapeDtypeStruct(u_piece.shape, jnp.bfloat16),
        in_specs=[SMEM, SMEM, ANY, ANY, VMEM] + [ANY] * len(parts),
        out_specs=VMEM,
        scratch_shapes=[
            pltpu.VMEM((count, depth, width), jnp.bfloat16),
            pltpu.VMEM((2 * half, rows, width), jnp.bfloat16),
            pltpu.SemaphoreType.DMA((len(parts),)),
            pltpu.SemaphoreType.DMA((2,)),
        ],
        compiler_params=pltpu.CompilerParams(vmem_limit_bytes=VMEM_LIMIT),
        name="project_out",
    )(slots, pos, near, far, u_piece, *parts)


def body(sizes, tokens, norm_gains, q_blocks, k_blocks, v_blocks, o_blocks, q_rows, k_rows, v_rows, o_rows, mask_blocks):
    sections, fsdp, tensor = sizes
    assert sections == 4 and tensor == 2
    pair_up = fsdp == 4
    send = lambda value, target: hop(value, sizes, target)
    p = lax.axis_index("pipe")
    z = lax.axis_index("fsdp")
    x = lax.axis_index("tensor")
    per, cols_half, shard, width = q_blocks.shape[1:]
    oper_t, cols_all = o_blocks.shape[1:3]
    cols = cols_half // sections
    rows = tokens.shape[0]
    feats = cols_all * width

    listed = jnp.concatenate([r.reshape(-1) for r in (q_rows, k_rows, v_rows, o_rows)]).astype(jnp.float32)
    packed = jnp.concatenate([norm_gains.reshape(-1), listed])
    shared = lax.all_gather(packed, ("pipe", "tensor"), axis=0).reshape(sections, tensor, -1)
    gains = shared[:, 0, :feats].reshape(sections, cols_all, 1, width)
    lists = shared[:, :, feats:].astype(jnp.int32)
    in_count = 3 * per * cols_half
    in_lists = lax.dynamic_index_in_dim(lists[:, :, :in_count], x, 1, keepdims=False)
    in_lists = in_lists.reshape(sections, 3, per, sections, cols)
    in_lists = lax.dynamic_index_in_dim(in_lists, p, 3, keepdims=False).reshape(sections, -1)
    out_lists = lists[:, :, in_count:].reshape(sections, tensor, oper_t, tensor, sections, cols)
    out_lists = lax.dynamic_index_in_dim(out_lists, x, 3, keepdims=False)
    out_lists = lax.dynamic_index_in_dim(out_lists, p, 3, keepdims=False)
    out_lists = out_lists + (jnp.arange(tensor) * cols_half)[:, None, None]
    out_lists = jnp.stack([lax.dynamic_index_in_dim(out_lists, x ^ j, 1, keepdims=False) for j in range(tensor)], 1)
    out_lists = out_lists.reshape(sections, -1)

    def slot_of(block):
        dx = (block // cols_half) ^ x
        d = ((block % cols_half) // cols) ^ p
        return (d & 1) * cols_half + (d >> 1) * (2 * cols) + dx * cols + block % cols

    in_slots = slot_of(in_lists)
    out_slots = slot_of(out_lists)
    slot = jnp.arange(cols_all)
    d = ((slot // (2 * cols)) % 2) * 2 + slot // cols_half
    block_at = (x ^ ((slot // cols) % 2)) * cols_half + (p ^ d) * cols + slot % cols
    gains = jnp.take(gains, block_at, axis=1)

    def in_piece(d):
        pieces = [
            lax.dynamic_slice_in_dim(w[0], (p ^ d) * cols, cols, 1).reshape(-1, shard, width)
            for w in (q_blocks, k_blocks, v_blocks)
        ]
        return jnp.concatenate(pieces, axis=0)

    own_in = in_piece(0)
    in_pieces = [None] * sections
    moved = {}
    for first in range(2):
        group = (first, first + 2)
        for d in (1, 2, 3):
            moved[first, d] = send(in_piece(d), lambda p, z, x: (p ^ d, z, x) if p in group else None)
        for s in group:
            in_pieces[s] = lax.select_n(p ^ s, own_in, *(moved[first, d] for d in (1, 2, 3)))

    o_split = o_blocks[0].reshape(oper_t, tensor, sections, cols, shard, width)
    o_own = lax.dynamic_index_in_dim(o_split, x, 1, keepdims=False)
    o_other = lax.dynamic_index_in_dim(o_split, 1 - x, 1, keepdims=False)
    o_other = send(o_other, lambda p, z, x: (p, z, 1 - x))
    o_all = jnp.stack([o_own, o_other])

    def out_piece(d):
        return lax.dynamic_index_in_dim(o_all, p ^ d, 2, keepdims=False).reshape(-1, shard, width)

    o_moved = [out_piece(0)] + [send(out_piece(d), lambda p, z, x: (p ^ d, z, x)) for d in (1, 2, 3)]
    out_pieces = [lax.select_n(p ^ s, *o_moved) for s in range(sections)]

    if pair_up:
        near_z = {0: 1, 3: 2}
        far_z = {0: 2, 3: 1}
        swap_z = {1: 2, 2: 1}
        back_z = {1: 0, 2: 3}
        step = lambda where: (lambda p, z, x: (p, where[z], x) if z in where else None)
        inner = (z == 1) | (z == 2)
        low = z < 2
        pos = jnp.where(low, jnp.array([1, 0, 2, 3]), jnp.array([2, 3, 1, 0])).astype(jnp.int32)
        chain = []

        def spread(piece):
            tie = chain[-1] if chain else ()
            piece = after(piece, *tie)
            swapped = send(piece, step(swap_z))
            near = send(piece, step(near_z))
            chain.append((swapped, near))
            far = send(after(piece, swapped, near), step(far_z))
            chain.append((far,))
            return [piece, near, swapped, far]
    else:
        pos = jnp.zeros((1,), jnp.int32)

        def spread(piece):
            return [lax.all_gather(piece, "fsdp", axis=1, tiled=True)]

    in_weights, out_weights = [], []
    for s in range(sections):
        in_weights.append(spread(in_pieces[s]))
        out_weights.append(spread(out_pieces[s]))

    piece = lax.dynamic_slice_in_dim(tokens, p * cols * width, cols * width, 1)
    piece = jnp.transpose(piece.reshape(rows, cols, width), (1, 0, 2))
    streams = [piece]
    masks = [mask_blocks]
    if pair_up:
        streams.append(send(piece, step(near_z)))
        masks.append(send(mask_blocks, step(near_z)))
    allow = [jnp.repeat(jnp.repeat(m, MBLK, axis=1), MBLK, axis=2).astype(jnp.float32) for m in masks]

    def share(value):
        by_x = send(value, lambda p, z, x: (p, z, 1 - x))
        by_y = send(value, lambda p, z, x: (p ^ 2, z, x))
        by_xy = send(value, lambda p, z, x: (p ^ 2, z, 1 - x))
        near = jnp.concatenate([value, by_x, by_y, by_xy], axis=0)
        far = send(near, lambda p, z, x: (p ^ 1, z, x))
        return near, far

    def half_rows(blocks):
        return jnp.concatenate(blocks, axis=0).transpose(1, 0, 2).reshape(rows, -1)

    results = [jnp.zeros((rows, cols_half * width), jnp.bfloat16) for _ in streams]
    for s in range(sections):
        for i, u in enumerate(streams):
            near, far = share(u)
            if s > 0:
                blocks = []
                for to in range(sections):
                    d = to ^ (s - 1)
                    blocks.append((far if d & 1 else near)[(d >> 1) * 2 * cols : (d >> 1) * 2 * cols + cols])
                results[i] = jnp.where(p == s - 1, half_rows(blocks), results[i])
            heads = attend(in_slots[s], pos, near, far, gains[s], allow[i], in_weights[s])
            near, far = share(heads)
            streams[i] = project_out(out_slots[s], pos, near, far, u, out_weights[s])

    last = sections - 1
    final = streams[0]
    result = results[0]
    if pair_up:
        final = jnp.where(inner, final, send(streams[1], step(back_z)))
        result = jnp.where(inner, result, send(results[1], step(back_z)))
    blocks = [None] * sections
    blocks[last] = final
    for d in (1, 2, 3):
        blocks[last ^ d] = send(final, lambda p, z, x: (last, z, x) if p == last ^ d else None)
    return jnp.where(p == last, half_rows(blocks), result)[None]


def solution(mesh):
    placed = (
        P("fsdp", "tensor"),
        P("pipe", None),
        P("pipe", None, "tensor", "fsdp", None),
        P("pipe", None, "tensor", "fsdp", None),
        P("pipe", None, "tensor", "fsdp", None),
        P("pipe", "tensor", None, "fsdp", None),
        P("pipe", None, "tensor"),
        P("pipe", None, "tensor"),
        P("pipe", None, "tensor"),
        P("pipe", "tensor", None),
        P("fsdp", None, None),
    )
    sizes = tuple(mesh.shape[axis] for axis in AXES)
    return jax.shard_map(
        functools.partial(body, sizes),
        mesh=mesh,
        in_specs=placed,
        out_specs=P("pipe", "fsdp", "tensor"),
        check_vma=False,
    )
```

```python
import functools

import jax
import jax.numpy as jnp
from jax import lax
from jax.experimental import pallas as pl
from jax.experimental.pallas import tpu as pltpu
from jax.sharding import PartitionSpec as P

HD = 128
MBLK = 16
ATTEND_US = 1
PROJECT_US = 1
AXES = ("pipe", "fsdp", "tensor")
VMEM_LIMIT = 24 * 1024 * 1024


def hop(value, sizes, target):
    pipe, fsdp, tensor = sizes
    pairs = []
    for p in range(pipe):
        for z in range(fsdp):
            for x in range(tensor):
                to = target(p, z, x)
                if to is not None:
                    pairs.append(((p * fsdp + z) * tensor + x, (to[0] * fsdp + to[1]) * tensor + to[2]))
    return lax.ppermute(value, AXES, pairs)


def after(value, *earlier):
    return lax.optimization_barrier((value, *earlier))[0]


def gather_weights(parts, firsts, total, sems, pos_ref):
    copies = []
    planes = len(parts) // 2
    for i, (part, first) in enumerate(zip(parts, firsts)):
        rows = part.shape[1]
        start = pl.multiple_of(pos_ref[i % planes] * rows, rows)
        copy = pltpu.make_async_copy(
            part.at[pl.ds(first, total.shape[1])], total.at[i // planes, :, pl.ds(start, rows), :], sems.at[i]
        )
        copy.start()
        copies.append(copy)
    return copies


def slot_of(block, me_ref, cols, blocks):
    half = blocks // 2
    dx = (block // half) ^ me_ref[1]
    d = ((block % half) // cols) ^ me_ref[0]
    piece = jnp.where((me_ref[0] & 1) == 1, 2 * dx + (d >> 1), (d & 2) + dx)
    return (piece * 2 + (d & 1)) * cols + block % cols


def attend_kernel(section, firsts, me_ref, list_ref, pos_ref, *rest):
    pieces, (gain_ref, allow_ref), parts = rest[:4], rest[4:6], rest[6 : 6 + len(firsts)]
    outs, (weights, normed, proj, sems) = rest[6 + len(firsts) : -4], rest[-4:]
    out_ref = outs[0]
    copies = gather_weights(parts, firsts, weights, sems, pos_ref)
    cols, (per_piece, rows, width) = out_ref.shape[0] // 2, pieces[0].shape
    blocks = 4 * per_piece
    row = me_ref[0] ^ section
    square = jnp.zeros((rows, width), jnp.float32)
    for piece in pieces:
        for t in range(per_piece):
            block = piece[t].astype(jnp.float32)
            square += block * block
    mean = jnp.sum(square, axis=-1, keepdims=True) / (blocks * width)
    inv_rms = lax.rsqrt(mean + 1e-05)
    for i, piece in enumerate(pieces):
        for t in range(per_piece):
            odd = me_ref[0] & 1
            dx = jnp.where(odd == 1, i // 2, i % 2)
            dy = jnp.where(odd == 1, i % 2, i // 2)
            place = ((me_ref[1] ^ dx) * (blocks // 2) + (me_ref[0] ^ (2 * dy + t // cols)) * cols + t % cols) * width
            gain = gain_ref[pl.ds(row, 1), pl.ds(pl.multiple_of(place, width), width)]
            normed[i * per_piece + t] = (piece[t].astype(jnp.float32) * inv_rms * gain).astype(jnp.bfloat16)
    if len(outs) > 1:
        keeper_y = (section - 1) // 2
        odd = me_ref[0] & 1
        for dy in range(2):
            for t in range(per_piece):
                place = ((keeper_y ^ dy) * per_piece + (odd ^ (t // cols)) * cols + t % cols) * width
                value = jnp.where(odd == 1, pieces[dy][t], pieces[2 * dy][t])
                outs[1][:, pl.ds(pl.multiple_of(place, width), width)] = value
    for copy in copies:
        copy.wait()
    count = weights.shape[1]
    per = count // (3 * cols)
    wide = blocks // 2
    for core in range(2):
        for kind in range(3):
            for c in range(cols):
                total = None
                for i in range(per):
                    n = (kind * per + i) * cols + c
                    where = (kind * per + i) * wide + (me_ref[0] ^ core) * cols + c
                    slot = slot_of(list_ref[row, where], me_ref, cols, blocks)
                    term = jnp.dot(normed[slot], weights[core, n], preferred_element_type=jnp.float32)
                    total = term if total is None else total + term
                proj[kind, core * cols + c] = total.astype(jnp.bfloat16)
    seq_len = allow_ref.shape[1]
    heads = [(c, pl.ds(h * HD, HD)) for c in range(2 * cols) for h in range(width // HD)]
    for n in range(allow_ref.shape[0]):
        span = pl.ds(n * seq_len, seq_len)
        scores = [
            lax.dot_general(
                proj[0, c, span, lanes],
                proj[1, c, span, lanes],
                (((1,), (1,)), ((), ())),
                preferred_element_type=jnp.float32,
            )
            for c, lanes in heads
        ]
        scores = jnp.stack(scores) * HD ** (-0.5)
        scores = jnp.where(allow_ref[n][None] > 0, scores, jnp.float32(-1e30))
        exp_scores = jnp.exp(scores - jnp.max(scores, axis=-1, keepdims=True))
        probs = (exp_scores / jnp.sum(exp_scores, axis=-1, keepdims=True)).astype(jnp.bfloat16)
        for i, (c, lanes) in enumerate(heads):
            attended = jnp.dot(probs[i], proj[2, c, span, lanes], preferred_element_type=jnp.float32)
            out_ref[c, span, lanes] = attended.astype(jnp.bfloat16)


def output_kernel(section, firsts, me_ref, list_ref, pos_ref, *rest):
    pieces, u_ref, parts = rest[:4], rest[4], rest[5 : 5 + len(firsts)]
    out_ref, weights, heads, sems, head_sems = rest[5 + len(firsts) :]
    copies = gather_weights(parts, firsts, weights, sems, pos_ref)
    per_piece = pieces[0].shape[0]
    for i, piece in enumerate(pieces):
        copy = pltpu.make_async_copy(piece, heads.at[pl.ds(i * per_piece, per_piece)], head_sems.at[i])
        copy.start()
        copies.append(copy)
    for copy in copies:
        copy.wait()
    blocks = 4 * per_piece
    cols = out_ref.shape[0] // 2
    count = weights.shape[1]
    per = count // cols
    wide = blocks // 2
    row = me_ref[0] ^ section
    for core in range(2):
        for c in range(cols):
            total = None
            for i in range(per):
                half = i // (per // 2)
                where = (i * 2 + me_ref[1]) * wide + (me_ref[0] ^ core) * cols + c
                block = list_ref[row, where] + (me_ref[1] ^ half) * wide
                slot = slot_of(block, me_ref, cols, blocks)
                term = jnp.dot(heads[slot], weights[core, i * cols + c], preferred_element_type=jnp.float32)
                total = term if total is None else total + term
            to = core * cols + c
            out_ref[to] = (u_ref[to].astype(jnp.float32) + total).astype(jnp.bfloat16)


SMEM = pl.BlockSpec(memory_space=pltpu.SMEM)
VMEM = pl.BlockSpec(memory_space=pltpu.VMEM)
ANY = pl.BlockSpec(memory_space=pl.ANY)


def hint(us):
    return pl.CostEstimate(flops=int(us * 1e9), bytes_accessed=0, transcendentals=0)


def attend(section, me, lists, pos, pieces, gains, allow, count, parts):
    cols, rows, width = pieces[0].shape
    depth = sum(part.shape[1] for part, _ in parts) // 2
    outs = [jax.ShapeDtypeStruct((cols, rows, width), jnp.bfloat16)]
    if section > 0:
        outs.append(jax.ShapeDtypeStruct((rows, 2 * cols * width), jnp.bfloat16))
    return pl.pallas_call(
        functools.partial(attend_kernel, section, tuple(first for _, first in parts)),
        out_shape=outs,
        in_specs=[SMEM] * 3 + [VMEM] * 6 + [ANY] * len(parts),
        out_specs=[VMEM] * len(outs),
        scratch_shapes=[
            pltpu.VMEM((2, count, depth, width), jnp.bfloat16),
            pltpu.VMEM((4 * cols, rows, width), jnp.bfloat16),
            pltpu.VMEM((3, cols, rows, width), jnp.bfloat16),
            pltpu.SemaphoreType.DMA((len(parts),)),
        ],
        compiler_params=pltpu.CompilerParams(vmem_limit_bytes=VMEM_LIMIT),
        cost_estimate=hint(ATTEND_US),
        name="attend",
    )(me, lists, pos, *pieces, gains, allow, *(part for part, _ in parts))


def project_out(section, me, lists, pos, pieces, u_piece, count, parts):
    cols, rows, width = u_piece.shape
    depth = sum(part.shape[1] for part, _ in parts) // 2
    return pl.pallas_call(
        functools.partial(output_kernel, section, tuple(first for _, first in parts)),
        out_shape=jax.ShapeDtypeStruct(u_piece.shape, jnp.bfloat16),
        in_specs=[SMEM] * 3 + [ANY] * 4 + [VMEM] + [ANY] * len(parts),
        out_specs=VMEM,
        scratch_shapes=[
            pltpu.VMEM((2, count, depth, width), jnp.bfloat16),
            pltpu.VMEM((4 * cols, rows, width), jnp.bfloat16),
            pltpu.SemaphoreType.DMA((len(parts),)),
            pltpu.SemaphoreType.DMA((4,)),
        ],
        compiler_params=pltpu.CompilerParams(vmem_limit_bytes=VMEM_LIMIT),
        cost_estimate=hint(PROJECT_US),
        name="project_out",
    )(me, lists, pos, *pieces, u_piece, *(part for part, _ in parts))


def body(sizes, tokens, norm_gains, q_blocks, k_blocks, v_blocks, o_blocks, q_rows, k_rows, v_rows, o_rows, mask_blocks):
    sections, fsdp, tensor = sizes
    assert sections == 4 and tensor == 2
    send = lambda value, target: hop(value, sizes, target)
    p = lax.axis_index("pipe")
    z = lax.axis_index("fsdp")
    x = lax.axis_index("tensor")
    per, cols_half, shard, width = q_blocks.shape[1:]
    oper_t, cols_all = o_blocks.shape[1:3]
    cols = cols_half // sections
    rows = tokens.shape[0]
    feats = cols_all * width

    to_x = lambda p, z, x: (p, z, 1 - x)
    to_core = lambda p, z, x: (p ^ 1, z, x)
    as_float = lambda r: r.reshape(-1).astype(jnp.float32)
    o_list = as_float(o_rows)
    packed = jnp.concatenate(
        [as_float(q_rows), as_float(k_rows), as_float(v_rows), o_list, send(o_list, to_x), norm_gains.reshape(-1)]
    )[None]
    packed = jnp.concatenate([packed, send(packed, lambda p, z, x: (p ^ 1, z, x))])
    packed = jnp.concatenate([packed, send(packed, lambda p, z, x: (p ^ 2, z, x))])
    in_end = 3 * per * cols_half
    list_end = in_end + tensor * oper_t * cols_all
    in_lists = packed[:, :in_end].astype(jnp.int32)
    out_lists = packed[:, in_end:list_end].astype(jnp.int32)
    gains = packed[:, list_end:]
    me = jnp.stack([p, x]).astype(jnp.int32)

    pair_up = fsdp == 4
    if pair_up:
        near_z = {0: 1, 3: 2}
        far_z = {0: 2, 3: 1}
        swap_z = {1: 2, 2: 1}
        back_z = {1: 0, 2: 3}
        step = lambda where: (lambda p, z, x: (p, where[z], x) if z in where else None)
        inner = (z == 1) | (z == 2)

    piece = tokens.reshape(rows, sections // 2, 2, cols, width)
    piece = lax.dynamic_index_in_dim(piece, p >> 1, 1, keepdims=False)
    piece = jnp.stack([lax.dynamic_index_in_dim(piece, (p & 1) ^ dc, 1, keepdims=False) for dc in range(2)])
    piece = jnp.transpose(piece, (0, 2, 1, 3)).reshape(2 * cols, rows, width)
    mask = mask_blocks
    if pair_up:
        odd_near = lambda p, z, x: (p, near_z[z], x) if p & 1 and z in near_z else None
        piece = jnp.where((p & 1) == 1, send(piece, odd_near), piece)
        mask = jnp.where((p & 1) == 1, send(mask, odd_near), mask)
    allow = jnp.repeat(jnp.repeat(mask, MBLK, axis=1), MBLK, axis=2).astype(jnp.float32)
    by_first = lambda p, z, x: (p ^ 2, z, x) if p & 1 else (p, z, 1 - x)
    by_second = lambda p, z, x: (p, z, 1 - x) if p & 1 else (p ^ 2, z, x)

    def share(value):
        first = send(value, by_first)
        return [value, first, send(value, by_second), send(first, by_second)]

    def in_piece(d):
        pieces = [
            lax.dynamic_slice_in_dim(w[0], (p ^ d) * cols, cols, 1).reshape(-1, shard, width)
            for w in (q_blocks, k_blocks, v_blocks)
        ]
        return jnp.concatenate(pieces, axis=0)

    own_in = in_piece(0)
    in_pieces = [None] * sections

    def exchange(group, *tie):
        moved = [
            send(after(in_piece(d), *tie) if tie else in_piece(d), lambda p, z, x: (p ^ d, z, x) if p in group else None)
            for d in (1, 2, 3)
        ]
        for s in group:
            in_pieces[s] = lax.select_n(p ^ s, own_in, *moved)
        return moved

    moved = exchange((0, 2))
    u = after(piece, *moved)
    pieces = share(u)
    o_split = o_blocks[0].reshape(oper_t, tensor, sections, cols, shard, width)
    o_own = lax.dynamic_index_in_dim(o_split, x, 1, keepdims=False)
    o_other = lax.dynamic_index_in_dim(o_split, 1 - x, 1, keepdims=False)
    o_other = send(o_other, to_x)
    o_all = after(jnp.stack([o_own, o_other]), *moved)

    def out_piece(d):
        return lax.dynamic_index_in_dim(o_all, p ^ d, 2, keepdims=False).reshape(-1, shard, width)

    o_moved = [out_piece(0)] + [send(out_piece(d), lambda p, z, x: (p ^ d, z, x)) for d in (1, 2, 3)]
    moved = exchange((1, 3), *o_moved[1:], *pieces[1:])
    out_pieces = [lax.select_n(p ^ s, *o_moved) for s in range(sections)]

    if pair_up:
        low = z < 2
        pos = jnp.where(low, jnp.array([1, 0, 2, 3]), jnp.array([2, 3, 1, 0])).astype(jnp.int32)

        def first_leg(piece, *tie):
            piece = after(piece, *tie)
            return [piece, send(piece, step(near_z)), send(piece, step(swap_z))]

        def second_leg(leg, late, *tie):
            far = send(after(leg[0], *leg[1:], *tie), step(far_z))
            return with_core(leg + [after(far, *late)]), far

        def all_legs(piece, *tie):
            leg = first_leg(piece, *tie)
            leg.append(send(leg[0], step(far_z)))
            return with_core(leg), leg[-1]
    else:
        pos = jnp.zeros((1,), jnp.int32)

        def first_leg(piece, *tie):
            return [lax.all_gather(piece, "fsdp", axis=1, tiled=True)]

        def second_leg(leg, late, *tie):
            return with_core(leg), leg[0]

        def all_legs(piece, *tie):
            leg = first_leg(piece)
            return with_core(leg), leg[0]

    def with_core(parts):
        return [(part, 0) for part in parts + [send(part, to_core) for part in parts]]

    in_count, out_count = in_pieces[0].shape[0], out_pieces[0].shape[0]

    def deliver(core):
        if not pair_up:
            return kept[core]
        return send(
            kept[core],
            lambda p, z, x: (p - (p & 1) + core, back_z[z] if p & 1 else z, x) if z in back_z else None,
        )

    kept = [None, None]
    results = [None, None]
    leg = first_leg(in_pieces[0])
    ready = after(out_pieces[0], *leg[1:])
    in_weights, last_far = second_leg(leg, moved, gains, allow, *pieces[1:])
    out_weights, out_far = all_legs(ready, *pieces[1:])
    pieces[0] = after(pieces[0], *(part for part, _ in out_weights))
    last_far = after(last_far, out_far)
    for s in range(sections):
        if s + 1 < sections:
            leg = first_leg(jnp.concatenate([in_pieces[s + 1], out_pieces[s + 1]]), last_far, u)
        if s > 0:
            pieces = share(u)
        heads, *before = attend(s, me, in_lists, pos, pieces, gains, allow, in_count, in_weights)
        if s + 1 < sections:
            parts, last_far = second_leg(leg, [], heads)
        if s > 0:
            core = (s - 1) & 1
            kept[core] = before[0] if kept[core] is None else jnp.where((p >> 1) == 0, kept[core], before[0])
        if s == sections - 1:
            results = [deliver(core) for core in range(2)]
        pieces = share(heads)
        if s == sections - 1:
            pieces[0] = after(pieces[0], *results)
        u = project_out(s, me, out_lists, pos, pieces, u, out_count, out_weights)
        if s + 1 < sections:
            in_weights, out_weights = parts, [(part, first + in_count) for part, first in parts]

    final = u
    last_core = (sections - 1) & 1
    if pair_up:
        home = lambda z, core: back_z[z] if core else z
    else:
        home = lambda z, core: z if core == last_core else None
    halves = []
    for y in range(2):

        def to_last(p, z, x, y=y):
            to = home(z, p & 1) if (p >> 1) == y and (not pair_up or z in back_z) else None
            return None if to is None else (sections - 1, to, x)

        halves.append(send(final, to_last))
    made_by = jnp.where(inner, 0, 1) if pair_up else last_core
    blocks = jnp.stack(halves).reshape(2, 2, cols, rows, width)
    blocks = jnp.where(made_by == 1, blocks[:, ::-1], blocks)
    last = jnp.transpose(blocks, (3, 0, 1, 2, 4)).reshape(rows, -1)
    result = jnp.where((p & 1) == 1, results[1], results[0])
    return jnp.where(p == sections - 1, last, result)[None]


def solution(mesh):
    placed = (
        P("fsdp", "tensor"),
        P("pipe", None),
        P("pipe", None, "tensor", "fsdp", None),
        P("pipe", None, "tensor", "fsdp", None),
        P("pipe", None, "tensor", "fsdp", None),
        P("pipe", "tensor", None, "fsdp", None),
        P("pipe", None, "tensor"),
        P("pipe", None, "tensor"),
        P("pipe", None, "tensor"),
        P("pipe", "tensor", None),
        P("fsdp", None, None),
    )
    sizes = tuple(mesh.shape[axis] for axis in AXES)
    return jax.shard_map(
        functools.partial(body, sizes),
        mesh=mesh,
        in_specs=placed,
        out_specs=P("pipe", "fsdp", "tensor"),
        check_vma=False,
    )
```

```python
import functools

import jax
import jax.numpy as jnp
from jax import lax
from jax.experimental import pallas as pl
from jax.experimental.pallas import tpu as pltpu
from jax.sharding import PartitionSpec as P

HD = 128
MBLK = 16
ATTEND_US = 1
PROJECT_US = 1
AXES = ("pipe", "fsdp", "tensor")
VMEM_LIMIT = 32 * 1024 * 1024
CUT_VMEM = 48 * 1024 * 1024
PICK_VMEM = 12 * 1024 * 1024


def hop(value, sizes, target):
    pipe, fsdp, tensor = sizes
    pairs = []
    for p in range(pipe):
        for z in range(fsdp):
            for x in range(tensor):
                to = target(p, z, x)
                if to is not None:
                    pairs.append(((p * fsdp + z) * tensor + x, (to[0] * fsdp + to[1]) * tensor + to[2]))
    return lax.ppermute(value, AXES, pairs)


def after(value, *earlier):
    return lax.optimization_barrier((value, *earlier))[0]


def weight_copies(parts, first, total, sems, pos_ref):
    copies = []
    for i, part in enumerate(parts):
        rows = part.shape[1]
        start = pl.multiple_of(pos_ref[i // 2] * rows, rows)
        source = part.at[pl.ds(first, total.shape[1])]
        copies.append(pltpu.make_async_copy(source, total.at[i % 2, :, pl.ds(start, rows), :], sems.at[i]))
    return copies


def slot_of(block, me_ref, cols, blocks):
    half = blocks // 2
    dx = (block // half) ^ me_ref[1]
    d = ((block % half) // cols) ^ me_ref[0]
    piece = jnp.where((me_ref[0] & 1) == 1, 2 * dx + (d >> 1), (d & 2) + dx)
    return (piece * 2 + (d & 1)) * cols + block % cols


def attend_kernel(section, n_parts, seq_len, me_ref, list_ref, pos_ref, mask_ref, *rest):
    pieces, gain_ref, parts = rest[:4], rest[4], rest[5 : 5 + n_parts]
    outs, (weights, normed, proj, sems) = rest[5 + n_parts : -4], rest[-4:]
    out_ref = outs[0]
    copies = weight_copies(parts, 0, weights, sems, pos_ref)
    for copy in copies:
        copy.start()
    cols, (per_piece, rows, width) = out_ref.shape[0] // 2, pieces[0].shape
    blocks = 4 * per_piece
    row = me_ref[0] ^ section
    first_gain = gain_ref.shape[1] - blocks * width
    square = jnp.zeros((rows, width), jnp.float32)
    for piece in pieces:
        for t in range(per_piece):
            block = piece[t].astype(jnp.float32)
            square += block * block
    mean = jnp.sum(square, axis=-1, keepdims=True) / (blocks * width)
    inv_rms = lax.rsqrt(mean + 1e-05)
    for i, piece in enumerate(pieces):
        for t in range(per_piece):
            odd = me_ref[0] & 1
            dx = jnp.where(odd == 1, i // 2, i % 2)
            dy = jnp.where(odd == 1, i % 2, i // 2)
            place = ((me_ref[1] ^ dx) * (blocks // 2) + (me_ref[0] ^ (2 * dy + t // cols)) * cols + t % cols) * width
            gain = gain_ref[pl.ds(row, 1), pl.ds(pl.multiple_of(first_gain + place, HD), width)]
            normed[i * per_piece + t] = (piece[t].astype(jnp.float32) * inv_rms * gain).astype(jnp.bfloat16)
    if len(outs) > 1:
        keeper_y = (section - 1) // 2
        odd = me_ref[0] & 1
        for dy in range(2):
            for t in range(per_piece):
                place = ((keeper_y ^ dy) * per_piece + (odd ^ (t // cols)) * cols + t % cols) * width
                value = jnp.where(odd == 1, pieces[dy][t], pieces[2 * dy][t])
                outs[1][:, pl.ds(pl.multiple_of(place, width), width)] = value
    for copy in copies:
        copy.wait()
    count = weights.shape[1]
    per = count // (3 * cols)
    wide = blocks // 2
    for core in range(2):
        for kind in range(3):
            for c in range(cols):
                total = None
                for i in range(per):
                    n = (kind * per + i) * cols + c
                    where = (kind * per + i) * wide + (me_ref[0] ^ core) * cols + c
                    slot = slot_of(list_ref[row, where].astype(jnp.int32), me_ref, cols, blocks)
                    term = jnp.dot(normed[slot], weights[core, n], preferred_element_type=jnp.float32)
                    total = term if total is None else total + term
                proj[kind, core * cols + c] = total.astype(jnp.bfloat16)
    heads = [(c, pl.ds(h * HD, HD)) for c in range(2 * cols) for h in range(width // HD)]
    along = seq_len // MBLK
    square_shape = (seq_len, seq_len)
    pair = (lax.broadcasted_iota(jnp.int32, square_shape, 0) // MBLK) * along
    pair = pair + lax.broadcasted_iota(jnp.int32, square_shape, 1) // MBLK
    for n in range(rows // seq_len):
        allowed = jnp.zeros(square_shape, jnp.int32)
        for i in range(along):
            for j in range(along):
                allowed = jnp.where(pair == i * along + j, mask_ref[n, i, j], allowed)
        span = pl.ds(n * seq_len, seq_len)
        scores = [
            lax.dot_general(
                proj[0, c, span, lanes],
                proj[1, c, span, lanes],
                (((1,), (1,)), ((), ())),
                preferred_element_type=jnp.float32,
            )
            for c, lanes in heads
        ]
        scores = jnp.stack(scores) * HD ** (-0.5)
        scores = jnp.where(allowed[None] == 1, scores, jnp.float32(-1e30))
        exp_scores = jnp.exp(scores - jnp.max(scores, axis=-1, keepdims=True))
        probs = (exp_scores / jnp.sum(exp_scores, axis=-1, keepdims=True)).astype(jnp.bfloat16)
        for i, (c, lanes) in enumerate(heads):
            attended = jnp.dot(probs[i], proj[2, c, span, lanes], preferred_element_type=jnp.float32)
            out_ref[c, span, lanes] = attended.astype(jnp.bfloat16)


def output_kernel(section, first, n_parts, list_first, me_ref, list_ref, other_ref, pos_ref, *rest):
    pieces, u_ref, parts = rest[:4], rest[4], rest[5 : 5 + n_parts]
    out_ref, weights, heads, sems, head_sems = rest[5 + n_parts :]
    copies = weight_copies(parts, first, weights, sems, pos_ref)
    per_piece = pieces[0].shape[0]
    for i, piece in enumerate(pieces):
        copy = pltpu.make_async_copy(piece, heads.at[pl.ds(i * per_piece, per_piece)], head_sems.at[i])
        copies.append(copy)
    for copy in copies:
        copy.start()
    for copy in copies:
        copy.wait()
    blocks = 4 * per_piece
    cols = out_ref.shape[0] // 2
    count = weights.shape[1]
    per = count // cols
    wide = blocks // 2
    row = me_ref[0] ^ section
    for core in range(2):
        for c in range(cols):
            total = None
            for i in range(per):
                half = i // (per // 2)
                where = list_first + ((i % (per // 2)) * 2 + me_ref[1]) * wide + (me_ref[0] ^ core) * cols + c
                block = (other_ref if half else list_ref)[row, where].astype(jnp.int32) + (me_ref[1] ^ half) * wide
                slot = slot_of(block, me_ref, cols, blocks)
                term = jnp.dot(heads[slot], weights[core, i * cols + c], preferred_element_type=jnp.float32)
                total = term if total is None else total + term
            to = core * cols + c
            out_ref[to] = (u_ref[to].astype(jnp.float32) + total).astype(jnp.bfloat16)


def cut_kernel(me_ref, *rest):
    blocks, outs, sems = rest[:4], rest[4:-1], rest[-1]
    p, x = me_ref[0], me_ref[1]
    cols_half = blocks[0].shape[2]
    cols = cols_half // len(outs)
    copies = []
    for d, out in enumerate(outs):
        at = 0
        for kind, ref in enumerate(blocks):
            first = (x * cols_half if kind == 3 else 0) + (p ^ d) * cols
            for i in range(ref.shape[1]):
                source = ref.at[0, i, pl.ds(first, cols)]
                copies.append(pltpu.make_async_copy(source, out.at[pl.ds(at, cols)], sems.at[len(copies)]))
                at += cols
    for copy in copies:
        copy.start()
    for copy in copies:
        copy.wait()


def prepare_kernel(oper_t, cols, me_ref, o_ref, token_ref, q_rows, k_rows, v_rows, o_rows, gain_ref, *rest):
    o_send, piece_ref, packed_ref, sems = rest
    p, x = me_ref[0], me_ref[1]
    cols_half = 4 * cols
    copies = []
    for d in range(4):
        for i in range(oper_t):
            to = o_send.at[pl.ds((d * oper_t + i) * cols, cols)]
            copies.append((o_ref.at[0, i, pl.ds((1 - x) * cols_half + (p ^ d) * cols, cols)], to))
    width = piece_ref.shape[2]
    for t in range(2 * cols):
        place = (((p >> 1) * 2 + ((p & 1) ^ (t // cols))) * cols + t % cols) * width
        copies.append((token_ref.at[:, pl.ds(pl.multiple_of(place, width), width)], piece_ref.at[t]))
    copies = [pltpu.make_async_copy(source, to, sems.at[i]) for i, (source, to) in enumerate(copies)]
    for copy in copies:
        copy.start()
    feats = gain_ref.shape[1]
    first = packed_ref.shape[1] - feats
    lane = lax.broadcasted_iota(jnp.int32, (1, first), 1)
    row = jnp.zeros((1, first), jnp.int32)
    at = 0
    for ref in (q_rows, k_rows, v_rows, o_rows):
        for i in range(ref.shape[1]):
            for c in range(ref.shape[2]):
                row = jnp.where(lane == at, ref[0, i, c], row)
                at += 1
    packed_ref[:, pl.ds(0, first)] = row.astype(jnp.float32)
    packed_ref[:, pl.ds(first, feats)] = gain_ref[...]
    for copy in copies:
        copy.wait()


def pick_kernel(choice, counts, me_ref, *rest):
    sources, (out, sems) = list(rest[:-2]), rest[-2:]
    copies = []
    for number, count in enumerate(counts):
        mine, sources = sources[:count], sources[count:]
        when = False
        for q, n in enumerate(choice):
            if n == number:
                when = (me_ref[0] == q) | when
        at = 0
        for j, source in enumerate(mine):
            size = source.shape[0]
            copies.append((when, pltpu.make_async_copy(source, out.at[pl.ds(at, size)], sems.at[j])))
            at += size
    for when, copy in copies:
        pl.when(when)(copy.start)
    for when, copy in copies:
        pl.when(when)(copy.wait)


SMEM = pl.BlockSpec(memory_space=pltpu.SMEM)
VMEM = pl.BlockSpec(memory_space=pltpu.VMEM)
ANY = pl.BlockSpec(memory_space=pl.ANY)


def hint(us):
    return pl.CostEstimate(flops=int(us * 1e9), bytes_accessed=0, transcendentals=0)


def attend(section, me, lists, gains, pos, mask, pieces, count, parts):
    cols, rows, width = pieces[0].shape
    depth = sum(part.shape[1] for part in parts) // 2
    outs = [jax.ShapeDtypeStruct((cols, rows, width), jnp.bfloat16)]
    if section > 0:
        outs.append(jax.ShapeDtypeStruct((rows, 2 * cols * width), jnp.bfloat16))
    return pl.pallas_call(
        functools.partial(attend_kernel, section, len(parts), rows // mask.shape[0]),
        out_shape=outs,
        in_specs=[SMEM] * 4 + [VMEM] * 5 + [ANY] * len(parts),
        out_specs=[VMEM] * len(outs),
        scratch_shapes=[
            pltpu.VMEM((2, count, depth, width), jnp.bfloat16),
            pltpu.VMEM((4 * cols, rows, width), jnp.bfloat16),
            pltpu.VMEM((3, cols, rows, width), jnp.bfloat16),
            pltpu.SemaphoreType.DMA((len(parts),)),
        ],
        compiler_params=pltpu.CompilerParams(vmem_limit_bytes=VMEM_LIMIT),
        cost_estimate=hint(ATTEND_US),
        name="attend",
    )(me, lists, pos, mask, *pieces, gains, *parts)


def project_out(section, me, lists, lists_x, list_first, pos, pieces, u_piece, first, count, parts):
    cols, rows, width = u_piece.shape
    depth = sum(part.shape[1] for part in parts) // 2
    return pl.pallas_call(
        functools.partial(output_kernel, section, first, len(parts), list_first),
        out_shape=jax.ShapeDtypeStruct(u_piece.shape, jnp.bfloat16),
        in_specs=[SMEM] * 4 + [ANY] * 4 + [VMEM] + [ANY] * len(parts),
        out_specs=VMEM,
        scratch_shapes=[
            pltpu.VMEM((2, count, depth, width), jnp.bfloat16),
            pltpu.VMEM((4 * cols, rows, width), jnp.bfloat16),
            pltpu.SemaphoreType.DMA((len(parts),)),
            pltpu.SemaphoreType.DMA((4,)),
        ],
        compiler_params=pltpu.CompilerParams(vmem_limit_bytes=VMEM_LIMIT),
        cost_estimate=hint(PROJECT_US),
        name="project_out",
    )(me, lists, lists_x, pos, *pieces, u_piece, *parts)


def cut(me, q_blocks, k_blocks, v_blocks, o_blocks):
    per, cols_half, shard, width = q_blocks.shape[1:]
    cols = cols_half // 4
    oper_t = o_blocks.shape[1]
    return pl.pallas_call(
        cut_kernel,
        out_shape=[jax.ShapeDtypeStruct(((3 * per + oper_t) * cols, shard, width), jnp.bfloat16)] * 4,
        in_specs=[SMEM] + [ANY] * 4,
        out_specs=[VMEM] * 4,
        scratch_shapes=[pltpu.SemaphoreType.DMA((4 * (3 * per + oper_t),))],
        compiler_params=pltpu.CompilerParams(vmem_limit_bytes=CUT_VMEM),
        cost_estimate=hint(1),
        name="cut",
    )(me, q_blocks, k_blocks, v_blocks, o_blocks)


def prepare(me, o_blocks, tokens, q_rows, k_rows, v_rows, o_rows, gains):
    oper_t, cols_all, shard, width = o_blocks.shape[1:]
    cols = cols_all // 8
    bf16 = lambda *shape: jax.ShapeDtypeStruct(shape, jnp.bfloat16)
    lists = sum(r.size for r in (q_rows, k_rows, v_rows, o_rows))
    lists += -lists % 128
    outs = [bf16(4 * oper_t * cols, shard, width), bf16(2 * cols, tokens.shape[0], width)]
    outs.append(jax.ShapeDtypeStruct((1, lists + gains.shape[1]), jnp.float32))
    return pl.pallas_call(
        functools.partial(prepare_kernel, oper_t, cols),
        out_shape=outs,
        in_specs=[SMEM] + [ANY] * 2 + [SMEM] * 4 + [VMEM],
        out_specs=[VMEM] * 3,
        scratch_shapes=[pltpu.SemaphoreType.DMA((4 * oper_t + 2 * cols,))],
        compiler_params=pltpu.CompilerParams(vmem_limit_bytes=PICK_VMEM),
        cost_estimate=hint(1),
        name="prepare",
    )(me, o_blocks, tokens, q_rows, k_rows, v_rows, o_rows, gains)


def pick(me, choice, candidates):
    used = sorted(set(choice))
    choice = tuple(used.index(n) for n in choice)
    candidates = [candidates[n] for n in used]
    first = candidates[0][0]
    size = sum(value.shape[0] for value in candidates[0])
    values = [value for candidate in candidates for value in candidate]
    return pl.pallas_call(
        functools.partial(pick_kernel, choice, tuple(len(candidate) for candidate in candidates)),
        out_shape=jax.ShapeDtypeStruct((size, *first.shape[1:]), first.dtype),
        in_specs=[SMEM] + [ANY] * len(values),
        out_specs=VMEM,
        scratch_shapes=[pltpu.SemaphoreType.DMA((max(len(candidate) for candidate in candidates),))],
        compiler_params=pltpu.CompilerParams(vmem_limit_bytes=PICK_VMEM),
        cost_estimate=hint(1),
        name="pick",
    )(me, *values)


def body(sizes, tokens, norm_gains, q_blocks, k_blocks, v_blocks, o_blocks, q_rows, k_rows, v_rows, o_rows, mask_blocks):
    sections, fsdp, tensor = sizes
    assert sections == 4 and tensor == 2
    send = lambda value, target: hop(value, sizes, target)
    p = lax.axis_index("pipe")
    z = lax.axis_index("fsdp")
    x = lax.axis_index("tensor")
    per, cols_half, shard, width = q_blocks.shape[1:]
    oper_t, cols_all = o_blocks.shape[1:3]
    cols = cols_half // sections
    rows = tokens.shape[0]
    feats = cols_all * width

    to_x = lambda p, z, x: (p, z, 1 - x)
    to_core = lambda p, z, x: (p ^ 1, z, x)
    to_pipe = lambda d: lambda p, z, x: (p ^ d, z, x)
    me = jnp.stack([p, x]).astype(jnp.int32)
    cut_for = cut(me, q_blocks, k_blocks, v_blocks, o_blocks)
    o_send, piece, packed = prepare(
        after(me, cut_for[2]), o_blocks, tokens, q_rows, k_rows, v_rows, o_rows, norm_gains
    )
    o_came = send(o_send, to_x)
    o_each = o_came.shape[0] // sections
    o_for = [o_came[d * o_each : (d + 1) * o_each] for d in range(sections)]
    packed = jnp.concatenate([packed] + [send(packed, to_pipe(d)) for d in (1, 2, 3)])
    lists = packed[:, : packed.shape[1] - norm_gains.shape[1]]

    pair_up = fsdp == 4
    if pair_up:
        near_z = {0: 1, 3: 2}
        far_z = {0: 2, 3: 1}
        swap_z = {1: 2, 2: 1}
        back_z = {1: 0, 2: 3}
        step = lambda where: (lambda p, z, x: (p, where[z], x) if z in where else None)
        inner = (z == 1) | (z == 2)

    mask = mask_blocks
    if pair_up:
        odd_near = lambda p, z, x: (p, near_z[z], x) if p & 1 and z in near_z else None
        piece = pick(me, (0, 1, 0, 1), [[piece], [send(piece, odd_near)]])
        mask = jnp.where((p & 1) == 1, send(mask, odd_near), mask)

    by_first = lambda p, z, x: (p ^ 2, z, x) if p & 1 else (p, z, 1 - x)
    by_second = lambda p, z, x: (p, z, 1 - x) if p & 1 else (p ^ 2, z, x)

    def share(value):
        first = send(value, by_first)
        return [value, first, send(value, by_second), send(first, by_second)]

    def exchange(values, ways):
        return {
            (d, pipes): [send(value, lambda p, z, x: (p ^ d, z, x) if p in pipes else None) for value in values[d]]
            for d, pipes in ways
        }

    def piece_of(section, came):
        keys = list(came)
        choice = []
        for q in range(sections):
            choice.append(next((i for i, (d, pipes) in enumerate(keys) if d == q ^ section and section in pipes), len(keys)))
        return pick(me, tuple(choice), [*came.values(), [cut_for[0], o_for[0]]])

    if pair_up:
        low = z < 2
        pos = jnp.where(low, jnp.array([1, 0, 2, 3]), jnp.array([2, 3, 1, 0])).astype(jnp.int32)

        def first_leg(piece, *tie):
            piece = after(piece, *tie) if tie else piece
            return [piece, send(piece, step(near_z)), send(piece, step(swap_z))]

        def second_leg(leg, *tie):
            return leg + [send(after(leg[0], *leg[1:], *tie), step(far_z))]

        def along_z(piece, tie=()):
            leg = first_leg(piece, *tie)
            return leg + [send(leg[0], step(far_z))]
    else:
        pos = jnp.zeros((1,), jnp.int32)

        def first_leg(piece, *tie):
            return [lax.all_gather(piece, "fsdp", axis=1, tiled=True)]

        def second_leg(leg, *tie):
            return leg

        def along_z(piece, tie=()):
            return [lax.all_gather(piece, "fsdp", axis=1, tiled=True)]

    def with_core(parts):
        return [each for part in parts for each in (part, send(part, to_core))]

    def deliver(core):
        if not pair_up:
            return kept[core]
        return send(
            kept[core],
            lambda p, z, x: (p - (p & 1) + core, back_z[z] if p & 1 else z, x) if z in back_z else None,
        )

    kept = [None, None]
    results = [None, None]
    o_for = [after(value, piece, mask) for value in o_for]
    round_a = exchange(list(zip(cut_for, o_for)), [(2, (0, 3)), (3, (0, 3)), (1, (0, 1, 2, 3))])
    leg = first_leg(piece_of(0, round_a))
    arrived = [value for values in list(round_a.values())[:2] for value in values]
    both_for = {d: [pick(me, (0,) * sections, [[after(cut_for[d], *arrived), o_for[d]]])] for d in (2, 3)}
    u = after(piece, *arrived)
    pieces = share(u)
    both_for = {d: [after(value, *pieces[1:]) for value in values] for d, values in both_for.items()}
    round_b = exchange(both_for, [(2, (1, 2)), (3, (1, 2))])
    round_b[1, (0, 1, 2, 3)] = round_a[1, (0, 1, 2, 3)]
    leg = second_leg(leg, pieces[1], packed)
    most = with_core(leg[:-1])
    in_count = 3 * per * cols
    out_count = leg[0].shape[0] - in_count
    lists_x = send(lists, to_x)
    for s in range(sections):
        last_leg = leg[-1:]
        if s > 0:
            pieces = share(u)
            last_leg = [after(part, pieces[1]) for part in last_leg]
        weights = most + with_core(last_leg)
        if s + 1 < sections:
            came = round_b if s + 1 in (1, 2) else round_a
            leg = first_leg(piece_of(s + 1, came), *last_leg)
        heads, *before = attend(s, me, lists, packed, pos, mask, pieces, in_count, weights)
        if s > 0:
            core = (s - 1) & 1
            kept[core] = before[0] if kept[core] is None else jnp.where((p >> 1) == 0, kept[core], before[0])
        if s == sections - 1:
            results = [deliver(core) for core in range(2)]
        pieces = share(heads)
        if s + 1 < sections:
            leg = second_leg(leg, *(pieces[1:] if s == 0 else pieces[1:2]))
            most = with_core(leg[:-1])
        if s == sections - 1:
            pieces[0] = after(pieces[0], *results)
        u = project_out(s, me, lists, lists_x, 3 * per * cols_half, pos, pieces, u, in_count, out_count, weights)

    final = u
    last_core = (sections - 1) & 1
    if pair_up:
        home = lambda z, core: back_z[z] if core else z
    else:
        home = lambda z, core: z if core == last_core else None
    halves = []
    for y in range(2):

        def to_last(p, z, x, y=y):
            to = home(z, p & 1) if (p >> 1) == y and (not pair_up or z in back_z) else None
            return None if to is None else (sections - 1, to, x)

        halves.append(send(final, to_last))
    made_by = jnp.where(inner, 0, 1) if pair_up else last_core
    blocks = jnp.stack(halves).reshape(2, 2, cols, rows, width)
    blocks = jnp.where(made_by == 1, blocks[:, ::-1], blocks)
    last = jnp.transpose(blocks, (3, 0, 1, 2, 4)).reshape(rows, -1)
    result = jnp.where((p & 1) == 1, results[1], results[0])
    return jnp.where(p == sections - 1, last, result)[None]


def solution(mesh):
    placed = (
        P("fsdp", "tensor"),
        P("pipe", None),
        P("pipe", None, "tensor", "fsdp", None),
        P("pipe", None, "tensor", "fsdp", None),
        P("pipe", None, "tensor", "fsdp", None),
        P("pipe", "tensor", None, "fsdp", None),
        P("pipe", None, "tensor"),
        P("pipe", None, "tensor"),
        P("pipe", None, "tensor"),
        P("pipe", "tensor", None),
        P("fsdp", None, None),
    )
    sizes = tuple(mesh.shape[axis] for axis in AXES)
    return jax.shard_map(
        functools.partial(body, sizes),
        mesh=mesh,
        in_specs=placed,
        out_specs=P("pipe", "fsdp", "tensor"),
        check_vma=False,
    )
```

```python
import functools

import jax
import jax.numpy as jnp
from jax import lax
from jax.experimental import pallas as pl
from jax.experimental.pallas import tpu as pltpu
from jax.sharding import PartitionSpec as P

HD = 128
MBLK = 16
ATTEND_US = 1
PROJECT_US = 1
AXES = ("pipe", "fsdp", "tensor")
VMEM_LIMIT = 32 * 1024 * 1024
CUT_VMEM = 48 * 1024 * 1024
PICK_VMEM = 12 * 1024 * 1024


def hop(value, sizes, target):
    pipe, fsdp, tensor = sizes
    pairs = []
    for p in range(pipe):
        for z in range(fsdp):
            for x in range(tensor):
                to = target(p, z, x)
                if to is not None:
                    pairs.append(((p * fsdp + z) * tensor + x, (to[0] * fsdp + to[1]) * tensor + to[2]))
    return lax.ppermute(value, AXES, pairs)


def after(value, *earlier):
    return lax.optimization_barrier((value, *earlier))[0]


def weight_copies(parts, first, total, sems, pos_ref):
    copies = []
    for i, part in enumerate(parts):
        rows = part.shape[1]
        start = pl.multiple_of(pos_ref[i // 2] * rows, rows)
        source = part.at[pl.ds(first, total.shape[1])]
        copies.append(pltpu.make_async_copy(source, total.at[i % 2, :, pl.ds(start, rows), :], sems.at[i]))
    return copies


def slot_of(block, me_ref, cols, blocks):
    half = blocks // 2
    dx = (block // half) ^ me_ref[1]
    d = ((block % half) // cols) ^ me_ref[0]
    piece = jnp.where((me_ref[0] & 1) == 1, 2 * dx + (d >> 1), (d & 2) + dx)
    return (piece * 2 + (d & 1)) * cols + block % cols


def attend_kernel(section, n_parts, seq_len, me_ref, list_ref, pos_ref, mask_ref, *rest):
    pieces, gain_ref, parts = rest[:4], rest[4], rest[5 : 5 + n_parts]
    outs, (weights, normed, proj, sems) = rest[5 + n_parts : -4], rest[-4:]
    out_ref = outs[0]
    copies = weight_copies(parts, 0, weights, sems, pos_ref)
    for copy in copies:
        copy.start()
    cols, (per_piece, rows, width) = out_ref.shape[0] // 2, pieces[0].shape
    blocks = 4 * per_piece
    row = me_ref[0] ^ section
    first_gain = gain_ref.shape[1] - blocks * width
    square = jnp.zeros((rows, width), jnp.float32)
    for piece in pieces:
        for t in range(per_piece):
            block = piece[t].astype(jnp.float32)
            square += block * block
    mean = jnp.sum(square, axis=-1, keepdims=True) / (blocks * width)
    inv_rms = lax.rsqrt(mean + 1e-05)
    for i, piece in enumerate(pieces):
        for t in range(per_piece):
            odd = me_ref[0] & 1
            dx = jnp.where(odd == 1, i // 2, i % 2)
            dy = jnp.where(odd == 1, i % 2, i // 2)
            place = ((me_ref[1] ^ dx) * (blocks // 2) + (me_ref[0] ^ (2 * dy + t // cols)) * cols + t % cols) * width
            gain = gain_ref[pl.ds(row, 1), pl.ds(pl.multiple_of(first_gain + place, HD), width)]
            normed[i * per_piece + t] = (piece[t].astype(jnp.float32) * inv_rms * gain).astype(jnp.bfloat16)
    if len(outs) > 1:
        keeper_y = (section - 1) // 2
        odd = me_ref[0] & 1
        for dy in range(2):
            for t in range(per_piece):
                place = ((keeper_y ^ dy) * per_piece + (odd ^ (t // cols)) * cols + t % cols) * width
                value = jnp.where(odd == 1, pieces[dy][t], pieces[2 * dy][t])
                outs[1][:, pl.ds(pl.multiple_of(place, width), width)] = value
    for copy in copies:
        copy.wait()
    count = weights.shape[1]
    per = count // (3 * cols)
    wide = blocks // 2
    for core in range(2):
        for kind in range(3):
            for c in range(cols):
                total = None
                for i in range(per):
                    n = (kind * per + i) * cols + c
                    where = (kind * per + i) * wide + (me_ref[0] ^ core) * cols + c
                    slot = slot_of(list_ref[row, where].astype(jnp.int32), me_ref, cols, blocks)
                    term = jnp.dot(normed[slot], weights[core, n], preferred_element_type=jnp.float32)
                    total = term if total is None else total + term
                proj[kind, core * cols + c] = total.astype(jnp.bfloat16)
    heads = [(c, pl.ds(h * HD, HD)) for c in range(2 * cols) for h in range(width // HD)]
    along = seq_len // MBLK
    square_shape = (seq_len, seq_len)
    pair = (lax.broadcasted_iota(jnp.int32, square_shape, 0) // MBLK) * along
    pair = pair + lax.broadcasted_iota(jnp.int32, square_shape, 1) // MBLK
    for n in range(rows // seq_len):
        allowed = jnp.zeros(square_shape, jnp.int32)
        for i in range(along):
            for j in range(along):
                allowed = jnp.where(pair == i * along + j, mask_ref[n, i, j], allowed)
        span = pl.ds(n * seq_len, seq_len)
        scores = [
            lax.dot_general(
                proj[0, c, span, lanes],
                proj[1, c, span, lanes],
                (((1,), (1,)), ((), ())),
                preferred_element_type=jnp.float32,
            )
            for c, lanes in heads
        ]
        scores = jnp.stack(scores) * HD ** (-0.5)
        scores = jnp.where(allowed[None] == 1, scores, jnp.float32(-1e30))
        exp_scores = jnp.exp(scores - jnp.max(scores, axis=-1, keepdims=True))
        probs = (exp_scores / jnp.sum(exp_scores, axis=-1, keepdims=True)).astype(jnp.bfloat16)
        for i, (c, lanes) in enumerate(heads):
            attended = jnp.dot(probs[i], proj[2, c, span, lanes], preferred_element_type=jnp.float32)
            out_ref[c, span, lanes] = attended.astype(jnp.bfloat16)


def output_kernel(section, first, n_parts, list_first, me_ref, list_ref, other_ref, pos_ref, *rest):
    pieces, u_ref, parts = rest[:4], rest[4], rest[5 : 5 + n_parts]
    out_ref, weights, heads, sems, head_sems = rest[5 + n_parts :]
    copies = weight_copies(parts, first, weights, sems, pos_ref)
    per_piece = pieces[0].shape[0]
    for i, piece in enumerate(pieces):
        copy = pltpu.make_async_copy(piece, heads.at[pl.ds(i * per_piece, per_piece)], head_sems.at[i])
        copies.append(copy)
    for copy in copies:
        copy.start()
    for copy in copies:
        copy.wait()
    blocks = 4 * per_piece
    cols = out_ref.shape[0] // 2
    count = weights.shape[1]
    per = count // cols
    wide = blocks // 2
    row = me_ref[0] ^ section
    for core in range(2):
        for c in range(cols):
            total = None
            for i in range(per):
                half = i // (per // 2)
                where = list_first + ((i % (per // 2)) * 2 + me_ref[1]) * wide + (me_ref[0] ^ core) * cols + c
                block = (other_ref if half else list_ref)[row, where].astype(jnp.int32) + (me_ref[1] ^ half) * wide
                slot = slot_of(block, me_ref, cols, blocks)
                term = jnp.dot(heads[slot], weights[core, i * cols + c], preferred_element_type=jnp.float32)
                total = term if total is None else total + term
            to = core * cols + c
            out_ref[to] = (u_ref[to].astype(jnp.float32) + total).astype(jnp.bfloat16)


def cut_kernel(me_ref, *rest):
    blocks, outs, sems = rest[:4], rest[4:-1], rest[-1]
    p, x = me_ref[0], me_ref[1]
    cols_half = blocks[0].shape[2]
    cols = cols_half // len(outs)
    copies = []
    for d, out in enumerate(outs):
        at = 0
        for kind, ref in enumerate(blocks):
            first = (x * cols_half if kind == 3 else 0) + (p ^ d) * cols
            for i in range(ref.shape[1]):
                source = ref.at[0, i, pl.ds(first, cols)]
                copies.append(pltpu.make_async_copy(source, out.at[pl.ds(at, cols)], sems.at[len(copies)]))
                at += cols
    for copy in copies:
        copy.start()
    for copy in copies:
        copy.wait()


def prepare_kernel(oper_t, cols, me_ref, o_ref, token_ref, q_rows, k_rows, v_rows, o_rows, gain_ref, *rest):
    o_send, piece_ref, packed_ref, sems = rest
    p, x = me_ref[0], me_ref[1]
    cols_half = 4 * cols
    copies = []
    for d in range(4):
        for i in range(oper_t):
            to = o_send.at[pl.ds((d * oper_t + i) * cols, cols)]
            copies.append((o_ref.at[0, i, pl.ds((1 - x) * cols_half + (p ^ d) * cols, cols)], to))
    width = piece_ref.shape[2]
    for t in range(2 * cols):
        place = (((p >> 1) * 2 + ((p & 1) ^ (t // cols))) * cols + t % cols) * width
        copies.append((token_ref.at[:, pl.ds(pl.multiple_of(place, width), width)], piece_ref.at[t]))
    copies = [pltpu.make_async_copy(source, to, sems.at[i]) for i, (source, to) in enumerate(copies)]
    for copy in copies:
        copy.start()
    feats = gain_ref.shape[1]
    first = packed_ref.shape[1] - feats
    lane = lax.broadcasted_iota(jnp.int32, (1, first), 1)
    row = jnp.zeros((1, first), jnp.int32)
    at = 0
    for ref in (q_rows, k_rows, v_rows, o_rows):
        for i in range(ref.shape[1]):
            for c in range(ref.shape[2]):
                row = jnp.where(lane == at, ref[0, i, c], row)
                at += 1
    packed_ref[:, pl.ds(0, first)] = row.astype(jnp.float32)
    packed_ref[:, pl.ds(first, feats)] = gain_ref[...]
    for copy in copies:
        copy.wait()


def pick_kernel(choice, counts, me_ref, *rest):
    sources, (out, sems) = list(rest[:-2]), rest[-2:]
    copies = []
    for number, count in enumerate(counts):
        mine, sources = sources[:count], sources[count:]
        when = False
        for q, n in enumerate(choice):
            if n == number:
                when = (me_ref[0] == q) | when
        at = 0
        for j, source in enumerate(mine):
            size = source.shape[0]
            copies.append((when, pltpu.make_async_copy(source, out.at[pl.ds(at, size)], sems.at[j])))
            at += size
    for when, copy in copies:
        pl.when(when)(copy.start)
    for when, copy in copies:
        pl.when(when)(copy.wait)


SMEM = pl.BlockSpec(memory_space=pltpu.SMEM)
VMEM = pl.BlockSpec(memory_space=pltpu.VMEM)
ANY = pl.BlockSpec(memory_space=pl.ANY)


def hint(us):
    return pl.CostEstimate(flops=int(us * 1e9), bytes_accessed=0, transcendentals=0)


def attend(section, me, lists, gains, pos, mask, pieces, count, parts):
    cols, rows, width = pieces[0].shape
    depth = sum(part.shape[1] for part in parts) // 2
    outs = [jax.ShapeDtypeStruct((cols, rows, width), jnp.bfloat16)]
    if section > 0:
        outs.append(jax.ShapeDtypeStruct((rows, 2 * cols * width), jnp.bfloat16))
    return pl.pallas_call(
        functools.partial(attend_kernel, section, len(parts), rows // mask.shape[0]),
        out_shape=outs,
        in_specs=[SMEM] * 4 + [VMEM] * 5 + [ANY] * len(parts),
        out_specs=[VMEM] * len(outs),
        scratch_shapes=[
            pltpu.VMEM((2, count, depth, width), jnp.bfloat16),
            pltpu.VMEM((4 * cols, rows, width), jnp.bfloat16),
            pltpu.VMEM((3, cols, rows, width), jnp.bfloat16),
            pltpu.SemaphoreType.DMA((len(parts),)),
        ],
        compiler_params=pltpu.CompilerParams(vmem_limit_bytes=VMEM_LIMIT),
        cost_estimate=hint(ATTEND_US),
        name="attend",
    )(me, lists, pos, mask, *pieces, gains, *parts)


def project_out(section, me, lists, lists_x, list_first, pos, pieces, u_piece, first, count, parts):
    cols, rows, width = u_piece.shape
    depth = sum(part.shape[1] for part in parts) // 2
    return pl.pallas_call(
        functools.partial(output_kernel, section, first, len(parts), list_first),
        out_shape=jax.ShapeDtypeStruct(u_piece.shape, jnp.bfloat16),
        in_specs=[SMEM] * 4 + [ANY] * 4 + [VMEM] + [ANY] * len(parts),
        out_specs=VMEM,
        scratch_shapes=[
            pltpu.VMEM((2, count, depth, width), jnp.bfloat16),
            pltpu.VMEM((4 * cols, rows, width), jnp.bfloat16),
            pltpu.SemaphoreType.DMA((len(parts),)),
            pltpu.SemaphoreType.DMA((4,)),
        ],
        compiler_params=pltpu.CompilerParams(vmem_limit_bytes=VMEM_LIMIT),
        cost_estimate=hint(PROJECT_US),
        name="project_out",
    )(me, lists, lists_x, pos, *pieces, u_piece, *parts)


def cut(me, q_blocks, k_blocks, v_blocks, o_blocks):
    per, cols_half, shard, width = q_blocks.shape[1:]
    cols = cols_half // 4
    oper_t = o_blocks.shape[1]
    return pl.pallas_call(
        cut_kernel,
        out_shape=[jax.ShapeDtypeStruct(((3 * per + oper_t) * cols, shard, width), jnp.bfloat16)] * 4,
        in_specs=[SMEM] + [ANY] * 4,
        out_specs=[VMEM] * 4,
        scratch_shapes=[pltpu.SemaphoreType.DMA((4 * (3 * per + oper_t),))],
        compiler_params=pltpu.CompilerParams(vmem_limit_bytes=CUT_VMEM),
        cost_estimate=hint(1),
        name="cut",
    )(me, q_blocks, k_blocks, v_blocks, o_blocks)


def prepare(me, o_blocks, tokens, q_rows, k_rows, v_rows, o_rows, gains):
    oper_t, cols_all, shard, width = o_blocks.shape[1:]
    cols = cols_all // 8
    bf16 = lambda *shape: jax.ShapeDtypeStruct(shape, jnp.bfloat16)
    lists = sum(r.size for r in (q_rows, k_rows, v_rows, o_rows))
    lists += -lists % 128
    outs = [bf16(4 * oper_t * cols, shard, width), bf16(2 * cols, tokens.shape[0], width)]
    outs.append(jax.ShapeDtypeStruct((1, lists + gains.shape[1]), jnp.float32))
    return pl.pallas_call(
        functools.partial(prepare_kernel, oper_t, cols),
        out_shape=outs,
        in_specs=[SMEM] + [ANY] * 2 + [SMEM] * 4 + [VMEM],
        out_specs=[VMEM] * 3,
        scratch_shapes=[pltpu.SemaphoreType.DMA((4 * oper_t + 2 * cols,))],
        compiler_params=pltpu.CompilerParams(vmem_limit_bytes=PICK_VMEM),
        cost_estimate=hint(1),
        name="prepare",
    )(me, o_blocks, tokens, q_rows, k_rows, v_rows, o_rows, gains)


def pick(me, choice, candidates):
    used = sorted(set(choice))
    choice = tuple(used.index(n) for n in choice)
    candidates = [candidates[n] for n in used]
    first = candidates[0][0]
    size = sum(value.shape[0] for value in candidates[0])
    values = [value for candidate in candidates for value in candidate]
    return pl.pallas_call(
        functools.partial(pick_kernel, choice, tuple(len(candidate) for candidate in candidates)),
        out_shape=jax.ShapeDtypeStruct((size, *first.shape[1:]), first.dtype),
        in_specs=[SMEM] + [ANY] * len(values),
        out_specs=VMEM,
        scratch_shapes=[pltpu.SemaphoreType.DMA((max(len(candidate) for candidate in candidates),))],
        compiler_params=pltpu.CompilerParams(vmem_limit_bytes=PICK_VMEM),
        cost_estimate=hint(1),
        name="pick",
    )(me, *values)


def body(sizes, tokens, norm_gains, q_blocks, k_blocks, v_blocks, o_blocks, q_rows, k_rows, v_rows, o_rows, mask_blocks):
    sections, fsdp, tensor = sizes
    assert sections == 4 and tensor == 2
    send = lambda value, target: hop(value, sizes, target)
    p = lax.axis_index("pipe")
    z = lax.axis_index("fsdp")
    x = lax.axis_index("tensor")
    per, cols_half, shard, width = q_blocks.shape[1:]
    oper_t, cols_all = o_blocks.shape[1:3]
    cols = cols_half // sections
    rows = tokens.shape[0]
    feats = cols_all * width

    to_x = lambda p, z, x: (p, z, 1 - x)
    to_core = lambda p, z, x: (p ^ 1, z, x)
    to_pipe = lambda d: lambda p, z, x: (p ^ d, z, x)
    me = jnp.stack([p, x]).astype(jnp.int32)
    cut_for = cut(me, q_blocks, k_blocks, v_blocks, o_blocks)
    o_send, piece, packed = prepare(
        after(me, cut_for[2]), o_blocks, tokens, q_rows, k_rows, v_rows, o_rows, norm_gains
    )
    o_came = send(o_send, to_x)
    o_each = o_came.shape[0] // sections
    o_for = [o_came[d * o_each : (d + 1) * o_each] for d in range(sections)]
    packed = jnp.concatenate([packed] + [send(packed, to_pipe(d)) for d in (1, 2, 3)])
    lists = packed[:, : packed.shape[1] - norm_gains.shape[1]]

    pair_up = fsdp == 4
    if pair_up:
        near_z = {0: 1, 3: 2}
        far_z = {0: 2, 3: 1}
        swap_z = {1: 2, 2: 1}
        back_z = {1: 0, 2: 3}
        step = lambda where: (lambda p, z, x: (p, where[z], x) if z in where else None)
        inner = (z == 1) | (z == 2)

    mask = mask_blocks
    if pair_up:
        odd_near = lambda p, z, x: (p, near_z[z], x) if p & 1 and z in near_z else None
        piece = pick(me, (0, 1, 0, 1), [[piece], [send(piece, odd_near)]])
        mask = jnp.where((p & 1) == 1, send(mask, odd_near), mask)

    by_first = lambda p, z, x: (p ^ 2, z, x) if p & 1 else (p, z, 1 - x)
    by_second = lambda p, z, x: (p, z, 1 - x) if p & 1 else (p ^ 2, z, x)

    def share(value):
        first, second = send(value, by_first), send(value, by_second)
        return [value, first, second, send(after(first, second), by_second)]

    def exchange(values, ways):
        return {
            (d, pipes): [send(value, lambda p, z, x: (p ^ d, z, x) if p in pipes else None) for value in values[d]]
            for d, pipes in ways
        }

    def piece_of(section, came):
        keys = list(came)
        choice = []
        for q in range(sections):
            choice.append(next((i for i, (d, pipes) in enumerate(keys) if d == q ^ section and section in pipes), len(keys)))
        return pick(me, tuple(choice), [*came.values(), [cut_for[0], o_for[0]]])

    if pair_up:
        low = z < 2
        pos = jnp.where(low, jnp.array([1, 0, 2, 3]), jnp.array([2, 3, 1, 0])).astype(jnp.int32)

        def first_leg(piece, *tie):
            piece = after(piece, *tie) if tie else piece
            swapped = send(piece, step(swap_z))
            return [piece, send(piece, step(near_z)), swapped]

        def second_leg(leg, *tie):
            return leg + [send(after(leg[0], *leg[1:], *tie), step(far_z))]

        def along_z(piece, tie=()):
            leg = first_leg(piece, *tie)
            return leg + [send(leg[0], step(far_z))]
    else:
        pos = jnp.zeros((1,), jnp.int32)

        def first_leg(piece, *tie):
            return [lax.all_gather(piece, "fsdp", axis=1, tiled=True)]

        def second_leg(leg, *tie):
            return leg

        def along_z(piece, tie=()):
            return [lax.all_gather(piece, "fsdp", axis=1, tiled=True)]

    def with_core(parts):
        return [each for part in parts for each in (part, send(part, to_core))]

    def deliver(core):
        if not pair_up:
            return kept[core]
        return send(
            kept[core],
            lambda p, z, x: (p - (p & 1) + core, back_z[z] if p & 1 else z, x) if z in back_z else None,
        )

    kept = [None, None]
    results = [None, None]
    o_for = [after(value, piece, mask) for value in o_for]
    round_a = exchange(list(zip(cut_for, o_for)), [(2, (0, 3)), (3, (0, 3)), (1, (0, 1, 2, 3))])
    leg = first_leg(piece_of(0, round_a))
    arrived = [value for values in list(round_a.values())[:2] for value in values]
    both_for = {d: [pick(me, (0,) * sections, [[after(cut_for[d], *arrived), o_for[d]]])] for d in (2, 3)}
    u = after(piece, *arrived)
    pieces = share(u)
    both_for = {d: [after(value, *pieces[1:]) for value in values] for d, values in both_for.items()}
    round_b = exchange(both_for, [(2, (1, 2)), (3, (1, 2))])
    round_b[1, (0, 1, 2, 3)] = round_a[1, (0, 1, 2, 3)]
    leg = second_leg(leg, pieces[1], packed)
    coming = None
    most = with_core(leg[:-1])
    in_count = 3 * per * cols
    out_count = leg[0].shape[0] - in_count
    lists_x = send(lists, to_x)
    for s in range(sections):
        last_leg = leg[-1:]
        if s > 0:
            pieces = share(u)
            last_leg = [after(part, pieces[3]) for part in last_leg]
        weights = most + with_core(last_leg)
        if s + 1 < sections:
            coming = piece_of(1, round_b) if s == 0 else coming
            leg = first_leg(coming, *last_leg)
        heads, *before = attend(s, me, lists, packed, pos, mask, pieces, in_count, weights)
        if s > 0:
            core = (s - 1) & 1
            kept[core] = before[0] if kept[core] is None else jnp.where((p >> 1) == 0, kept[core], before[0])
        if s == sections - 1:
            results = [deliver(core) for core in range(2)]
        pieces = share(heads)
        if s + 1 < sections:
            tie = pieces[1:]
            if s + 2 < sections:
                coming = piece_of(s + 2, round_b if s == 0 else round_a)
                tie = [*tie, coming]
            leg = second_leg(leg, *tie)
            most = with_core(leg[:-1])
        if s == sections - 1:
            pieces[0] = after(pieces[0], *results)
        u = project_out(s, me, lists, lists_x, 3 * per * cols_half, pos, pieces, u, in_count, out_count, weights)

    final = u
    last_core = (sections - 1) & 1
    if pair_up:
        home = lambda z, core: back_z[z] if core else z
    else:
        home = lambda z, core: z if core == last_core else None
    halves = []
    for y in range(2):

        def to_last(p, z, x, y=y):
            to = home(z, p & 1) if (p >> 1) == y and (not pair_up or z in back_z) else None
            return None if to is None else (sections - 1, to, x)

        halves.append(send(final, to_last))
    made_by = jnp.where(inner, 0, 1) if pair_up else last_core
    blocks = jnp.stack(halves).reshape(2, 2, cols, rows, width)
    blocks = jnp.where(made_by == 1, blocks[:, ::-1], blocks)
    last = jnp.transpose(blocks, (3, 0, 1, 2, 4)).reshape(rows, -1)
    result = jnp.where((p & 1) == 1, results[1], results[0])
    return jnp.where(p == sections - 1, last, result)[None]


def solution(mesh):
    placed = (
        P("fsdp", "tensor"),
        P("pipe", None),
        P("pipe", None, "tensor", "fsdp", None),
        P("pipe", None, "tensor", "fsdp", None),
        P("pipe", None, "tensor", "fsdp", None),
        P("pipe", "tensor", None, "fsdp", None),
        P("pipe", None, "tensor"),
        P("pipe", None, "tensor"),
        P("pipe", None, "tensor"),
        P("pipe", "tensor", None),
        P("fsdp", None, None),
    )
    sizes = tuple(mesh.shape[axis] for axis in AXES)
    return jax.shard_map(
        functools.partial(body, sizes),
        mesh=mesh,
        in_specs=placed,
        out_specs=P("pipe", "fsdp", "tensor"),
        check_vma=False,
    )
```

```python
import functools

import jax
import jax.numpy as jnp
from jax import lax
from jax.experimental import pallas as pl
from jax.experimental.pallas import tpu as pltpu
from jax.sharding import PartitionSpec as P

HD = 128
MBLK = 16
ATTEND_US = 1
PROJECT_US = 1
AXES = ("pipe", "fsdp", "tensor")
VMEM_LIMIT = 32 * 1024 * 1024
CUT_VMEM = 56 * 1024 * 1024
PICK_VMEM = 12 * 1024 * 1024


def hop(value, sizes, target):
    pipe, fsdp, tensor = sizes
    pairs = []
    for p in range(pipe):
        for z in range(fsdp):
            for x in range(tensor):
                to = target(p, z, x)
                if to is not None:
                    pairs.append(((p * fsdp + z) * tensor + x, (to[0] * fsdp + to[1]) * tensor + to[2]))
    return lax.ppermute(value, AXES, pairs)


def after(value, *earlier):
    return lax.optimization_barrier((value, *earlier))[0]


def weight_copies(parts, first, total, sems, pos_ref):
    copies = []
    for i, part in enumerate(parts):
        rows = part.shape[1]
        start = pl.multiple_of(pos_ref[i // 2] * rows, rows)
        source = part.at[pl.ds(first, total.shape[1])]
        copies.append(pltpu.make_async_copy(source, total.at[i % 2, :, pl.ds(start, rows), :], sems.at[i]))
    return copies


def slot_of(block, me_ref, cols, blocks):
    half = blocks // 2
    dx = (block // half) ^ me_ref[1]
    d = ((block % half) // cols) ^ me_ref[0]
    piece = jnp.where((me_ref[0] & 1) == 1, 2 * dx + (d >> 1), (d & 2) + dx)
    return (piece * 2 + (d & 1)) * cols + block % cols


def attend_kernel(section, n_parts, seq_len, me_ref, list_ref, pos_ref, mask_ref, *rest):
    pieces, gain_ref, parts = rest[:4], rest[4], rest[5 : 5 + n_parts]
    outs, (weights, normed, proj, sems) = rest[5 + n_parts : -4], rest[-4:]
    out_ref = outs[0]
    copies = weight_copies(parts, 0, weights, sems, pos_ref)
    for copy in copies:
        copy.start()
    cols, (per_piece, rows, width) = out_ref.shape[0] // 2, pieces[0].shape
    blocks = 4 * per_piece
    row = me_ref[0] ^ section
    first_gain = gain_ref.shape[1] - blocks * width
    square = jnp.zeros((rows, width), jnp.float32)
    for piece in pieces:
        for t in range(per_piece):
            block = piece[t].astype(jnp.float32)
            square += block * block
    mean = jnp.sum(square, axis=-1, keepdims=True) / (blocks * width)
    inv_rms = lax.rsqrt(mean + 1e-05)
    for i, piece in enumerate(pieces):
        for t in range(per_piece):
            odd = me_ref[0] & 1
            dx = jnp.where(odd == 1, i // 2, i % 2)
            dy = jnp.where(odd == 1, i % 2, i // 2)
            place = ((me_ref[1] ^ dx) * (blocks // 2) + (me_ref[0] ^ (2 * dy + t // cols)) * cols + t % cols) * width
            gain = gain_ref[pl.ds(row, 1), pl.ds(pl.multiple_of(first_gain + place, HD), width)]
            normed[i * per_piece + t] = (piece[t].astype(jnp.float32) * inv_rms * gain).astype(jnp.bfloat16)
    if len(outs) > 1:
        keeper_y = (section - 1) // 2
        odd = me_ref[0] & 1
        for dy in range(2):
            for t in range(per_piece):
                place = ((keeper_y ^ dy) * per_piece + (odd ^ (t // cols)) * cols + t % cols) * width
                value = jnp.where(odd == 1, pieces[dy][t], pieces[2 * dy][t])
                outs[1][:, pl.ds(pl.multiple_of(place, width), width)] = value
    for copy in copies:
        copy.wait()
    count = weights.shape[1]
    per = count // (3 * cols)
    wide = blocks // 2
    for core in range(2):
        for kind in range(3):
            for c in range(cols):
                total = None
                for i in range(per):
                    n = (kind * per + i) * cols + c
                    where = (kind * per + i) * wide + (me_ref[0] ^ core) * cols + c
                    slot = slot_of(list_ref[row, where].astype(jnp.int32), me_ref, cols, blocks)
                    term = jnp.dot(normed[slot], weights[core, n], preferred_element_type=jnp.float32)
                    total = term if total is None else total + term
                proj[kind, core * cols + c] = total.astype(jnp.bfloat16)
    heads = [(c, pl.ds(h * HD, HD)) for c in range(2 * cols) for h in range(width // HD)]
    along = seq_len // MBLK
    square_shape = (seq_len, seq_len)
    pair = (lax.broadcasted_iota(jnp.int32, square_shape, 0) // MBLK) * along
    pair = pair + lax.broadcasted_iota(jnp.int32, square_shape, 1) // MBLK
    for n in range(rows // seq_len):
        allowed = jnp.zeros(square_shape, jnp.int32)
        for i in range(along):
            for j in range(along):
                allowed = jnp.where(pair == i * along + j, mask_ref[n, i, j], allowed)
        span = pl.ds(n * seq_len, seq_len)
        scores = [
            lax.dot_general(
                proj[0, c, span, lanes],
                proj[1, c, span, lanes],
                (((1,), (1,)), ((), ())),
                preferred_element_type=jnp.float32,
            )
            for c, lanes in heads
        ]
        scores = jnp.stack(scores) * HD ** (-0.5)
        scores = jnp.where(allowed[None] == 1, scores, jnp.float32(-1e30))
        exp_scores = jnp.exp(scores - jnp.max(scores, axis=-1, keepdims=True))
        probs = (exp_scores / jnp.sum(exp_scores, axis=-1, keepdims=True)).astype(jnp.bfloat16)
        for i, (c, lanes) in enumerate(heads):
            attended = jnp.dot(probs[i], proj[2, c, span, lanes], preferred_element_type=jnp.float32)
            out_ref[c, span, lanes] = attended.astype(jnp.bfloat16)


def output_kernel(section, first, n_parts, list_first, me_ref, list_ref, other_ref, pos_ref, *rest):
    pieces, u_ref, parts = rest[:4], rest[4], rest[5 : 5 + n_parts]
    out_ref, weights, heads, sems, head_sems = rest[5 + n_parts :]
    copies = weight_copies(parts, first, weights, sems, pos_ref)
    per_piece = pieces[0].shape[0]
    for i, piece in enumerate(pieces):
        copy = pltpu.make_async_copy(piece, heads.at[pl.ds(i * per_piece, per_piece)], head_sems.at[i])
        copies.append(copy)
    for copy in copies:
        copy.start()
    for copy in copies:
        copy.wait()
    blocks = 4 * per_piece
    cols = out_ref.shape[0] // 2
    count = weights.shape[1]
    per = count // cols
    wide = blocks // 2
    row = me_ref[0] ^ section
    for core in range(2):
        for c in range(cols):
            total = None
            for i in range(per):
                half = i // (per // 2)
                where = list_first + ((i % (per // 2)) * 2 + me_ref[1]) * wide + (me_ref[0] ^ core) * cols + c
                block = (other_ref if half else list_ref)[row, where].astype(jnp.int32) + (me_ref[1] ^ half) * wide
                slot = slot_of(block, me_ref, cols, blocks)
                term = jnp.dot(heads[slot], weights[core, i * cols + c], preferred_element_type=jnp.float32)
                total = term if total is None else total + term
            to = core * cols + c
            out_ref[to] = (u_ref[to].astype(jnp.float32) + total).astype(jnp.bfloat16)


def cut_kernel(me_ref, *rest):
    blocks, outs, sems = rest[:4], rest[4:-1], rest[-1]
    p, x = me_ref[0], me_ref[1]
    cols_half = blocks[0].shape[2]
    cols = cols_half // len(outs)
    copies = []
    for d, out in enumerate(outs):
        at = 0
        for kind, ref in enumerate(blocks):
            first = (x * cols_half if kind == 3 else 0) + (p ^ d) * cols
            for i in range(ref.shape[1]):
                source = ref.at[0, i, pl.ds(first, cols)]
                copies.append(pltpu.make_async_copy(source, out.at[pl.ds(at, cols)], sems.at[len(copies)]))
                at += cols
    for copy in copies:
        copy.start()
    for copy in copies:
        copy.wait()


def prepare_kernel(oper_t, cols, me_ref, o_ref, token_ref, q_rows, k_rows, v_rows, o_rows, gain_ref, *rest):
    o_send, piece_ref, packed_ref, sems = rest
    p, x = me_ref[0], me_ref[1]
    cols_half = 4 * cols
    copies = []
    for d in range(4):
        for i in range(oper_t):
            to = o_send.at[pl.ds((d * oper_t + i) * cols, cols)]
            copies.append((o_ref.at[0, i, pl.ds((1 - x) * cols_half + (p ^ d) * cols, cols)], to))
    width = piece_ref.shape[2]
    for t in range(2 * cols):
        place = (((p >> 1) * 2 + ((p & 1) ^ (t // cols))) * cols + t % cols) * width
        copies.append((token_ref.at[:, pl.ds(pl.multiple_of(place, width), width)], piece_ref.at[t]))
    copies = [pltpu.make_async_copy(source, to, sems.at[i]) for i, (source, to) in enumerate(copies)]
    for copy in copies:
        copy.start()
    feats = gain_ref.shape[1]
    first = packed_ref.shape[1] - feats
    lane = lax.broadcasted_iota(jnp.int32, (1, first), 1)
    row = jnp.zeros((1, first), jnp.int32)
    at = 0
    for ref in (q_rows, k_rows, v_rows, o_rows):
        for i in range(ref.shape[1]):
            for c in range(ref.shape[2]):
                row = jnp.where(lane == at, ref[0, i, c], row)
                at += 1
    packed_ref[:, pl.ds(0, first)] = row.astype(jnp.float32)
    packed_ref[:, pl.ds(first, feats)] = gain_ref[...]
    for copy in copies:
        copy.wait()


def pick_kernel(choice, counts, me_ref, *rest):
    sources, (out, sems) = list(rest[:-2]), rest[-2:]
    copies = []
    for number, count in enumerate(counts):
        mine, sources = sources[:count], sources[count:]
        when = False
        for q, n in enumerate(choice):
            if n == number:
                when = (me_ref[0] == q) | when
        at = 0
        for j, source in enumerate(mine):
            size = source.shape[0]
            copies.append((when, pltpu.make_async_copy(source, out.at[pl.ds(at, size)], sems.at[j])))
            at += size
    for when, copy in copies:
        pl.when(when)(copy.start)
    for when, copy in copies:
        pl.when(when)(copy.wait)


SMEM = pl.BlockSpec(memory_space=pltpu.SMEM)
VMEM = pl.BlockSpec(memory_space=pltpu.VMEM)
ANY = pl.BlockSpec(memory_space=pl.ANY)


def hint(us):
    return pl.CostEstimate(flops=int(us * 1e9), bytes_accessed=0, transcendentals=0)


def attend(section, me, lists, gains, pos, mask, pieces, count, parts):
    cols, rows, width = pieces[0].shape
    depth = sum(part.shape[1] for part in parts) // 2
    outs = [jax.ShapeDtypeStruct((cols, rows, width), jnp.bfloat16)]
    if section > 0:
        outs.append(jax.ShapeDtypeStruct((rows, 2 * cols * width), jnp.bfloat16))
    return pl.pallas_call(
        functools.partial(attend_kernel, section, len(parts), rows // mask.shape[0]),
        out_shape=outs,
        in_specs=[SMEM] * 4 + [VMEM] * 5 + [ANY] * len(parts),
        out_specs=[VMEM] * len(outs),
        scratch_shapes=[
            pltpu.VMEM((2, count, depth, width), jnp.bfloat16),
            pltpu.VMEM((4 * cols, rows, width), jnp.bfloat16),
            pltpu.VMEM((3, cols, rows, width), jnp.bfloat16),
            pltpu.SemaphoreType.DMA((len(parts),)),
        ],
        compiler_params=pltpu.CompilerParams(vmem_limit_bytes=VMEM_LIMIT),
        cost_estimate=hint(ATTEND_US),
        name="attend",
    )(me, lists, pos, mask, *pieces, gains, *parts)


def project_out(section, me, lists, lists_x, list_first, pos, pieces, u_piece, first, count, parts):
    cols, rows, width = u_piece.shape
    depth = sum(part.shape[1] for part in parts) // 2
    return pl.pallas_call(
        functools.partial(output_kernel, section, first, len(parts), list_first),
        out_shape=jax.ShapeDtypeStruct(u_piece.shape, jnp.bfloat16),
        in_specs=[SMEM] * 4 + [ANY] * 4 + [VMEM] + [ANY] * len(parts),
        out_specs=VMEM,
        scratch_shapes=[
            pltpu.VMEM((2, count, depth, width), jnp.bfloat16),
            pltpu.VMEM((4 * cols, rows, width), jnp.bfloat16),
            pltpu.SemaphoreType.DMA((len(parts),)),
            pltpu.SemaphoreType.DMA((4,)),
        ],
        compiler_params=pltpu.CompilerParams(vmem_limit_bytes=VMEM_LIMIT),
        cost_estimate=hint(PROJECT_US),
        name="project_out",
    )(me, lists, lists_x, pos, *pieces, u_piece, *parts)


def cut(me, q_blocks, k_blocks, v_blocks, o_blocks):
    per, cols_half, shard, width = q_blocks.shape[1:]
    cols = cols_half // 4
    oper_t = o_blocks.shape[1]
    return pl.pallas_call(
        cut_kernel,
        out_shape=[jax.ShapeDtypeStruct(((3 * per + oper_t) * cols, shard, width), jnp.bfloat16)] * 4,
        in_specs=[SMEM] + [ANY] * 4,
        out_specs=[VMEM] * 4,
        scratch_shapes=[pltpu.SemaphoreType.DMA((4 * (3 * per + oper_t),))],
        compiler_params=pltpu.CompilerParams(vmem_limit_bytes=CUT_VMEM),
        cost_estimate=hint(1),
        name="cut",
    )(me, q_blocks, k_blocks, v_blocks, o_blocks)


def prepare(me, o_blocks, tokens, q_rows, k_rows, v_rows, o_rows, gains):
    oper_t, cols_all, shard, width = o_blocks.shape[1:]
    cols = cols_all // 8
    bf16 = lambda *shape: jax.ShapeDtypeStruct(shape, jnp.bfloat16)
    lists = sum(r.size for r in (q_rows, k_rows, v_rows, o_rows))
    lists += -lists % 128
    outs = [bf16(4 * oper_t * cols, shard, width), bf16(2 * cols, tokens.shape[0], width)]
    outs.append(jax.ShapeDtypeStruct((1, lists + gains.shape[1]), jnp.float32))
    return pl.pallas_call(
        functools.partial(prepare_kernel, oper_t, cols),
        out_shape=outs,
        in_specs=[SMEM] + [ANY] * 2 + [SMEM] * 4 + [VMEM],
        out_specs=[VMEM] * 3,
        scratch_shapes=[pltpu.SemaphoreType.DMA((4 * oper_t + 2 * cols,))],
        compiler_params=pltpu.CompilerParams(vmem_limit_bytes=PICK_VMEM),
        cost_estimate=hint(1),
        name="prepare",
    )(me, o_blocks, tokens, q_rows, k_rows, v_rows, o_rows, gains)


def pick(me, choice, candidates):
    used = sorted(set(choice))
    choice = tuple(used.index(n) for n in choice)
    candidates = [candidates[n] for n in used]
    first = candidates[0][0]
    size = sum(value.shape[0] for value in candidates[0])
    values = [value for candidate in candidates for value in candidate]
    return pl.pallas_call(
        functools.partial(pick_kernel, choice, tuple(len(candidate) for candidate in candidates)),
        out_shape=jax.ShapeDtypeStruct((size, *first.shape[1:]), first.dtype),
        in_specs=[SMEM] + [ANY] * len(values),
        out_specs=VMEM,
        scratch_shapes=[pltpu.SemaphoreType.DMA((max(len(candidate) for candidate in candidates),))],
        compiler_params=pltpu.CompilerParams(vmem_limit_bytes=PICK_VMEM),
        cost_estimate=hint(1),
        name="pick",
    )(me, *values)


def body(sizes, tokens, norm_gains, q_blocks, k_blocks, v_blocks, o_blocks, q_rows, k_rows, v_rows, o_rows, mask_blocks):
    sections, fsdp, tensor = sizes
    assert sections == 4 and tensor == 2
    send = lambda value, target: hop(value, sizes, target)
    p = lax.axis_index("pipe")
    z = lax.axis_index("fsdp")
    x = lax.axis_index("tensor")
    per, cols_half, shard, width = q_blocks.shape[1:]
    oper_t, cols_all = o_blocks.shape[1:3]
    cols = cols_half // sections
    rows = tokens.shape[0]
    feats = cols_all * width

    to_x = lambda p, z, x: (p, z, 1 - x)
    to_core = lambda p, z, x: (p ^ 1, z, x)
    to_pipe = lambda d: lambda p, z, x: (p ^ d, z, x)
    me = jnp.stack([p, x]).astype(jnp.int32)
    cut_for = cut(me, q_blocks, k_blocks, v_blocks, o_blocks)
    o_send, piece, packed = prepare(
        after(me, cut_for[2]), o_blocks, tokens, q_rows, k_rows, v_rows, o_rows, norm_gains
    )
    o_came = send(o_send, to_x)
    o_each = o_came.shape[0] // sections
    o_for = [o_came[d * o_each : (d + 1) * o_each] for d in range(sections)]
    packed = jnp.concatenate([packed] + [send(packed, to_pipe(d)) for d in (1, 2, 3)])
    lists = packed[:, : packed.shape[1] - norm_gains.shape[1]]

    pair_up = fsdp == 4
    if pair_up:
        near_z = {0: 1, 3: 2}
        far_z = {0: 2, 3: 1}
        swap_z = {1: 2, 2: 1}
        back_z = {1: 0, 2: 3}
        step = lambda where: (lambda p, z, x: (p, where[z], x) if z in where else None)
        inner = (z == 1) | (z == 2)

    mask = mask_blocks
    if pair_up:
        odd_near = lambda p, z, x: (p, near_z[z], x) if p & 1 and z in near_z else None
        piece = pick(me, (0, 1, 0, 1), [[piece], [send(piece, odd_near)]])
        mask = jnp.where((p & 1) == 1, send(mask, odd_near), mask)

    by_first = lambda p, z, x: (p ^ 2, z, x) if p & 1 else (p, z, 1 - x)
    by_second = lambda p, z, x: (p, z, 1 - x) if p & 1 else (p ^ 2, z, x)

    def share(value):
        first, second = send(value, by_first), send(value, by_second)
        return [value, first, second, send(after(first, second), by_second)]

    def exchange(values, ways):
        return {
            (d, pipes): [send(value, lambda p, z, x: (p ^ d, z, x) if p in pipes else None) for value in values[d]]
            for d, pipes in ways
        }

    def piece_of(section, came):
        keys = list(came)
        choice = []
        for q in range(sections):
            choice.append(next((i for i, (d, pipes) in enumerate(keys) if d == q ^ section and section in pipes), len(keys)))
        return pick(me, tuple(choice), [*came.values(), [cut_for[0], o_for[0]]])

    if pair_up:
        low = z < 2
        pos = jnp.where(low, jnp.array([1, 0, 2, 3]), jnp.array([2, 3, 1, 0])).astype(jnp.int32)

        def first_leg(piece, *tie):
            piece = after(piece, *tie) if tie else piece
            swapped = send(piece, step(swap_z))
            return [piece, send(piece, step(near_z)), swapped]

        def second_leg(leg, *tie):
            return leg + [send(after(leg[0], *leg[1:], *tie), step(far_z))]

        def along_z(piece, tie=()):
            leg = first_leg(piece, *tie)
            return leg + [send(leg[0], step(far_z))]
    else:
        pos = jnp.zeros((1,), jnp.int32)

        def first_leg(piece, *tie):
            return [lax.all_gather(piece, "fsdp", axis=1, tiled=True)]

        def second_leg(leg, *tie):
            return leg

        def along_z(piece, tie=()):
            return [lax.all_gather(piece, "fsdp", axis=1, tiled=True)]

    def with_core(parts):
        return [each for part in parts for each in (part, send(part, to_core))]

    def deliver(core):
        if not pair_up:
            return kept[core]
        return send(
            kept[core],
            lambda p, z, x: (p - (p & 1) + core, back_z[z] if p & 1 else z, x) if z in back_z else None,
        )

    kept = [None, None]
    results = [None, None]
    o_for = [after(value, piece, mask) for value in o_for]
    round_a = exchange(list(zip(cut_for, o_for)), [(2, (0, 3)), (3, (0, 3)), (1, (0, 1, 2, 3))])
    leg = first_leg(piece_of(0, round_a))
    arrived = [value for values in list(round_a.values())[:2] for value in values]
    both_for = {d: [pick(me, (0,) * sections, [[after(cut_for[d], *arrived), o_for[d]]])] for d in (2, 3)}
    u = after(piece, *arrived)
    pieces = share(u)
    both_for = {d: [after(value, *pieces[1:]) for value in values] for d, values in both_for.items()}
    round_b = exchange(both_for, [(2, (1, 2)), (3, (1, 2))])
    round_b[1, (0, 1, 2, 3)] = round_a[1, (0, 1, 2, 3)]
    leg = second_leg(leg, pieces[1], packed)
    coming = None
    most = with_core(leg[:-1])
    in_count = 3 * per * cols
    out_count = leg[0].shape[0] - in_count
    lists_x = send(lists, to_x)
    for s in range(sections):
        last_leg = leg[-1:]
        if s > 0:
            pieces = share(u)
            last_leg = [after(part, pieces[3]) for part in last_leg]
        weights = most + with_core(last_leg)
        if s + 1 < sections:
            coming = piece_of(1, round_b) if s == 0 else coming
            leg = first_leg(coming, *last_leg)
        heads, *before = attend(s, me, lists, packed, pos, mask, pieces, in_count, weights)
        if s > 0:
            core = (s - 1) & 1
            kept[core] = before[0] if kept[core] is None else jnp.where((p >> 1) == 0, kept[core], before[0])
        if s == sections - 1:
            results = [deliver(core) for core in range(2)]
        pieces = share(heads)
        if s + 1 < sections:
            tie = pieces[1:3] if s == 0 else pieces[1:]
            if s + 2 < sections:
                coming = piece_of(s + 2, round_b if s == 0 else round_a)
                tie = [*tie, coming]
            leg = second_leg(leg, *tie)
            most = with_core(leg[:-1])
        if s == sections - 1:
            result = jnp.where((p & 1) == 1, results[1], results[0])
            pieces[0] = after(pieces[0], result)
        u = project_out(s, me, lists, lists_x, 3 * per * cols_half, pos, pieces, u, in_count, out_count, weights)

    final = u
    last_core = (sections - 1) & 1
    if pair_up:
        home = lambda z, core: back_z[z] if core else z
    else:
        home = lambda z, core: z if core == last_core else None
    halves = []
    for y in range(2):

        def to_last(p, z, x, y=y):
            to = home(z, p & 1) if (p >> 1) == y and (not pair_up or z in back_z) else None
            return None if to is None else (sections - 1, to, x)

        halves.append(send(final, to_last))
    made_by = jnp.where(inner, 0, 1) if pair_up else last_core
    blocks = jnp.stack(halves).reshape(2, 2, cols, rows, width)
    blocks = jnp.where(made_by == 1, blocks[:, ::-1], blocks)
    last = jnp.transpose(blocks, (3, 0, 1, 2, 4)).reshape(rows, -1)
    return jnp.where(p == sections - 1, last, result)[None]


def solution(mesh):
    placed = (
        P("fsdp", "tensor"),
        P("pipe", None),
        P("pipe", None, "tensor", "fsdp", None),
        P("pipe", None, "tensor", "fsdp", None),
        P("pipe", None, "tensor", "fsdp", None),
        P("pipe", "tensor", None, "fsdp", None),
        P("pipe", None, "tensor"),
        P("pipe", None, "tensor"),
        P("pipe", None, "tensor"),
        P("pipe", "tensor", None),
        P("fsdp", None, None),
    )
    sizes = tuple(mesh.shape[axis] for axis in AXES)
    return jax.shard_map(
        functools.partial(body, sizes),
        mesh=mesh,
        in_specs=placed,
        out_specs=P("pipe", "fsdp", "tensor"),
        check_vma=False,
    )
```

```python
import functools

import jax
import jax.numpy as jnp
from jax import lax
from jax.experimental import pallas as pl
from jax.experimental.pallas import tpu as pltpu
from jax.sharding import PartitionSpec as P

HD = 128
MBLK = 16
ATTEND_US = 1
PROJECT_US = 1
AXES = ("pipe", "fsdp", "tensor")
VMEM_LIMIT = 32 * 1024 * 1024
CUT_VMEM = 56 * 1024 * 1024
PICK_VMEM = 12 * 1024 * 1024


def hop(value, sizes, target):
    pipe, fsdp, tensor = sizes
    pairs = []
    for p in range(pipe):
        for z in range(fsdp):
            for x in range(tensor):
                to = target(p, z, x)
                if to is not None:
                    pairs.append(((p * fsdp + z) * tensor + x, (to[0] * fsdp + to[1]) * tensor + to[2]))
    return lax.ppermute(value, AXES, pairs)


def after(value, *earlier):
    return lax.optimization_barrier((value, *earlier))[0]


def weight_copies(parts, first, total, sems, pos_ref):
    copies = []
    for i, part in enumerate(parts):
        rows = part.shape[1]
        start = pl.multiple_of(pos_ref[i // 2] * rows, rows)
        source = part.at[pl.ds(first, total.shape[1])]
        copies.append(pltpu.make_async_copy(source, total.at[i % 2, :, pl.ds(start, rows), :], sems.at[i]))
    return copies


def slot_of(block, me_ref, cols, blocks):
    half = blocks // 2
    dx = (block // half) ^ me_ref[1]
    d = ((block % half) // cols) ^ me_ref[0]
    piece = jnp.where((me_ref[0] & 1) == 1, 2 * dx + (d >> 1), (d & 2) + dx)
    return (piece * 2 + (d & 1)) * cols + block % cols


def attend_kernel(section, n_parts, seq_len, me_ref, list_ref, pos_ref, mask_ref, *rest):
    pieces, gain_ref, parts = rest[:4], rest[4], rest[5 : 5 + n_parts]
    outs, (weights, normed, proj, sems) = rest[5 + n_parts : -4], rest[-4:]
    out_ref = outs[0]
    each = weights.shape[1] // 3
    copies = [
        weight_copies(parts, kind * each, weights.at[:, pl.ds(kind * each, each)], sems.at[kind], pos_ref)
        for kind in range(3)
    ]
    for of_kind in copies:
        for copy in of_kind:
            copy.start()
    cols, (per_piece, rows, width) = out_ref.shape[0] // 2, pieces[0].shape
    blocks = 4 * per_piece
    row = me_ref[0] ^ section
    first_gain = gain_ref.shape[1] - blocks * width
    square = jnp.zeros((rows, width), jnp.float32)
    for piece in pieces:
        for t in range(per_piece):
            block = piece[t].astype(jnp.float32)
            square += block * block
    mean = jnp.sum(square, axis=-1, keepdims=True) / (blocks * width)
    inv_rms = lax.rsqrt(mean + 1e-05)
    for i, piece in enumerate(pieces):
        for t in range(per_piece):
            odd = me_ref[0] & 1
            dx = jnp.where(odd == 1, i // 2, i % 2)
            dy = jnp.where(odd == 1, i % 2, i // 2)
            place = ((me_ref[1] ^ dx) * (blocks // 2) + (me_ref[0] ^ (2 * dy + t // cols)) * cols + t % cols) * width
            gain = gain_ref[pl.ds(row, 1), pl.ds(pl.multiple_of(first_gain + place, HD), width)]
            normed[i * per_piece + t] = (piece[t].astype(jnp.float32) * inv_rms * gain).astype(jnp.bfloat16)
    if len(outs) > 1:
        keeper_y = (section - 1) // 2
        odd = me_ref[0] & 1
        for dy in range(2):
            for t in range(per_piece):
                place = ((keeper_y ^ dy) * per_piece + (odd ^ (t // cols)) * cols + t % cols) * width
                value = jnp.where(odd == 1, pieces[dy][t], pieces[2 * dy][t])
                outs[1][:, pl.ds(pl.multiple_of(place, width), width)] = value
    count = weights.shape[1]
    per = count // (3 * cols)
    wide = blocks // 2
    for kind in range(3):
        for copy in copies[kind]:
            copy.wait()
        for core in range(2):
            for c in range(cols):
                total = None
                for i in range(per):
                    n = (kind * per + i) * cols + c
                    where = (kind * per + i) * wide + (me_ref[0] ^ core) * cols + c
                    slot = slot_of(list_ref[row, where].astype(jnp.int32), me_ref, cols, blocks)
                    term = jnp.dot(normed[slot], weights[core, n], preferred_element_type=jnp.float32)
                    total = term if total is None else total + term
                proj[kind, core * cols + c] = total.astype(jnp.bfloat16)
    heads = [(c, pl.ds(h * HD, HD)) for c in range(2 * cols) for h in range(width // HD)]
    along = seq_len // MBLK
    square_shape = (seq_len, seq_len)
    pair = (lax.broadcasted_iota(jnp.int32, square_shape, 0) // MBLK) * along
    pair = pair + lax.broadcasted_iota(jnp.int32, square_shape, 1) // MBLK
    for n in range(rows // seq_len):
        allowed = jnp.zeros(square_shape, jnp.int32)
        for i in range(along):
            for j in range(along):
                allowed = jnp.where(pair == i * along + j, mask_ref[n, i, j], allowed)
        span = pl.ds(n * seq_len, seq_len)
        scores = [
            lax.dot_general(
                proj[0, c, span, lanes],
                proj[1, c, span, lanes],
                (((1,), (1,)), ((), ())),
                preferred_element_type=jnp.float32,
            )
            for c, lanes in heads
        ]
        scores = jnp.stack(scores) * HD ** (-0.5)
        scores = jnp.where(allowed[None] == 1, scores, jnp.float32(-1e30))
        exp_scores = jnp.exp(scores - jnp.max(scores, axis=-1, keepdims=True))
        probs = (exp_scores / jnp.sum(exp_scores, axis=-1, keepdims=True)).astype(jnp.bfloat16)
        for i, (c, lanes) in enumerate(heads):
            attended = jnp.dot(probs[i], proj[2, c, span, lanes], preferred_element_type=jnp.float32)
            out_ref[c, span, lanes] = attended.astype(jnp.bfloat16)


def output_kernel(section, first, n_parts, list_first, me_ref, list_ref, other_ref, pos_ref, *rest):
    pieces, u_ref, parts = rest[:4], rest[4], rest[5 : 5 + n_parts]
    out_ref, weights, heads, sems, head_sems = rest[5 + n_parts :]
    copies = weight_copies(parts, first, weights, sems, pos_ref)
    per_piece = pieces[0].shape[0]
    for i, piece in enumerate(pieces):
        copy = pltpu.make_async_copy(piece, heads.at[pl.ds(i * per_piece, per_piece)], head_sems.at[i])
        copies.append(copy)
    for copy in copies:
        copy.start()
    for copy in copies:
        copy.wait()
    blocks = 4 * per_piece
    cols = out_ref.shape[0] // 2
    count = weights.shape[1]
    per = count // cols
    wide = blocks // 2
    row = me_ref[0] ^ section
    for core in range(2):
        for c in range(cols):
            total = None
            for i in range(per):
                half = i // (per // 2)
                where = list_first + ((i % (per // 2)) * 2 + me_ref[1]) * wide + (me_ref[0] ^ core) * cols + c
                block = (other_ref if half else list_ref)[row, where].astype(jnp.int32) + (me_ref[1] ^ half) * wide
                slot = slot_of(block, me_ref, cols, blocks)
                term = jnp.dot(heads[slot], weights[core, i * cols + c], preferred_element_type=jnp.float32)
                total = term if total is None else total + term
            to = core * cols + c
            out_ref[to] = (u_ref[to].astype(jnp.float32) + total).astype(jnp.bfloat16)


def cut_kernel(me_ref, *rest):
    blocks, outs, sems = rest[:4], rest[4:-1], rest[-1]
    p, x = me_ref[0], me_ref[1]
    cols_half = blocks[0].shape[2]
    cols = cols_half // len(outs)
    copies = []
    for d, out in enumerate(outs):
        at = 0
        for kind, ref in enumerate(blocks):
            first = (x * cols_half if kind == 3 else 0) + (p ^ d) * cols
            for i in range(ref.shape[1]):
                source = ref.at[0, i, pl.ds(first, cols)]
                copies.append(pltpu.make_async_copy(source, out.at[pl.ds(at, cols)], sems.at[len(copies)]))
                at += cols
    for copy in copies:
        copy.start()
    for copy in copies:
        copy.wait()


def prepare_kernel(oper_t, cols, me_ref, o_ref, token_ref, q_rows, k_rows, v_rows, o_rows, gain_ref, *rest):
    o_send, piece_ref, packed_ref, sems = rest
    p, x = me_ref[0], me_ref[1]
    cols_half = 4 * cols
    copies = []
    for d in range(4):
        for i in range(oper_t):
            to = o_send.at[pl.ds((d * oper_t + i) * cols, cols)]
            copies.append((o_ref.at[0, i, pl.ds((1 - x) * cols_half + (p ^ d) * cols, cols)], to))
    width = piece_ref.shape[2]
    for t in range(2 * cols):
        place = (((p >> 1) * 2 + ((p & 1) ^ (t // cols))) * cols + t % cols) * width
        copies.append((token_ref.at[:, pl.ds(pl.multiple_of(place, width), width)], piece_ref.at[t]))
    copies = [pltpu.make_async_copy(source, to, sems.at[i]) for i, (source, to) in enumerate(copies)]
    for copy in copies:
        copy.start()
    feats = gain_ref.shape[1]
    first = packed_ref.shape[1] - feats
    lane = lax.broadcasted_iota(jnp.int32, (1, first), 1)
    row = jnp.zeros((1, first), jnp.int32)
    at = 0
    for ref in (q_rows, k_rows, v_rows, o_rows):
        for i in range(ref.shape[1]):
            for c in range(ref.shape[2]):
                row = jnp.where(lane == at, ref[0, i, c], row)
                at += 1
    packed_ref[:, pl.ds(0, first)] = row.astype(jnp.float32)
    packed_ref[:, pl.ds(first, feats)] = gain_ref[...]
    for copy in copies:
        copy.wait()


def pick_kernel(choice, counts, me_ref, *rest):
    sources, (out, sems) = list(rest[:-2]), rest[-2:]
    copies = []
    for number, count in enumerate(counts):
        mine, sources = sources[:count], sources[count:]
        when = False
        for q, n in enumerate(choice):
            if n == number:
                when = (me_ref[0] == q) | when
        at = 0
        for j, source in enumerate(mine):
            size = source.shape[0]
            copies.append((when, pltpu.make_async_copy(source, out.at[pl.ds(at, size)], sems.at[j])))
            at += size
    for when, copy in copies:
        pl.when(when)(copy.start)
    for when, copy in copies:
        pl.when(when)(copy.wait)


SMEM = pl.BlockSpec(memory_space=pltpu.SMEM)
VMEM = pl.BlockSpec(memory_space=pltpu.VMEM)
ANY = pl.BlockSpec(memory_space=pl.ANY)


def hint(us):
    return pl.CostEstimate(flops=int(us * 1e9), bytes_accessed=0, transcendentals=0)


def attend(section, me, lists, gains, pos, mask, pieces, count, parts):
    cols, rows, width = pieces[0].shape
    depth = sum(part.shape[1] for part in parts) // 2
    outs = [jax.ShapeDtypeStruct((cols, rows, width), jnp.bfloat16)]
    if section > 0:
        outs.append(jax.ShapeDtypeStruct((rows, 2 * cols * width), jnp.bfloat16))
    return pl.pallas_call(
        functools.partial(attend_kernel, section, len(parts), rows // mask.shape[0]),
        out_shape=outs,
        in_specs=[SMEM] * 4 + [VMEM] * 5 + [ANY] * len(parts),
        out_specs=[VMEM] * len(outs),
        scratch_shapes=[
            pltpu.VMEM((2, count, depth, width), jnp.bfloat16),
            pltpu.VMEM((4 * cols, rows, width), jnp.bfloat16),
            pltpu.VMEM((3, cols, rows, width), jnp.bfloat16),
            pltpu.SemaphoreType.DMA((3, len(parts))),
        ],
        compiler_params=pltpu.CompilerParams(vmem_limit_bytes=VMEM_LIMIT),
        cost_estimate=hint(ATTEND_US),
        name="attend",
    )(me, lists, pos, mask, *pieces, gains, *parts)


def project_out(section, me, lists, lists_x, list_first, pos, pieces, u_piece, first, count, parts):
    cols, rows, width = u_piece.shape
    depth = sum(part.shape[1] for part in parts) // 2
    return pl.pallas_call(
        functools.partial(output_kernel, section, first, len(parts), list_first),
        out_shape=jax.ShapeDtypeStruct(u_piece.shape, jnp.bfloat16),
        in_specs=[SMEM] * 4 + [ANY] * 4 + [VMEM] + [ANY] * len(parts),
        out_specs=VMEM,
        scratch_shapes=[
            pltpu.VMEM((2, count, depth, width), jnp.bfloat16),
            pltpu.VMEM((4 * cols, rows, width), jnp.bfloat16),
            pltpu.SemaphoreType.DMA((len(parts),)),
            pltpu.SemaphoreType.DMA((4,)),
        ],
        compiler_params=pltpu.CompilerParams(vmem_limit_bytes=VMEM_LIMIT),
        cost_estimate=hint(PROJECT_US),
        name="project_out",
    )(me, lists, lists_x, pos, *pieces, u_piece, *parts)


def cut(me, q_blocks, k_blocks, v_blocks, o_blocks):
    per, cols_half, shard, width = q_blocks.shape[1:]
    cols = cols_half // 4
    oper_t = o_blocks.shape[1]
    return pl.pallas_call(
        cut_kernel,
        out_shape=[jax.ShapeDtypeStruct(((3 * per + oper_t) * cols, shard, width), jnp.bfloat16)] * 4,
        in_specs=[SMEM] + [ANY] * 4,
        out_specs=[VMEM] * 4,
        scratch_shapes=[pltpu.SemaphoreType.DMA((4 * (3 * per + oper_t),))],
        compiler_params=pltpu.CompilerParams(vmem_limit_bytes=CUT_VMEM),
        cost_estimate=hint(1),
        name="cut",
    )(me, q_blocks, k_blocks, v_blocks, o_blocks)


def prepare(me, o_blocks, tokens, q_rows, k_rows, v_rows, o_rows, gains):
    oper_t, cols_all, shard, width = o_blocks.shape[1:]
    cols = cols_all // 8
    bf16 = lambda *shape: jax.ShapeDtypeStruct(shape, jnp.bfloat16)
    lists = sum(r.size for r in (q_rows, k_rows, v_rows, o_rows))
    lists += -lists % 128
    outs = [bf16(4 * oper_t * cols, shard, width), bf16(2 * cols, tokens.shape[0], width)]
    outs.append(jax.ShapeDtypeStruct((1, lists + gains.shape[1]), jnp.float32))
    return pl.pallas_call(
        functools.partial(prepare_kernel, oper_t, cols),
        out_shape=outs,
        in_specs=[SMEM] + [ANY] * 2 + [SMEM] * 4 + [VMEM],
        out_specs=[VMEM] * 3,
        scratch_shapes=[pltpu.SemaphoreType.DMA((4 * oper_t + 2 * cols,))],
        compiler_params=pltpu.CompilerParams(vmem_limit_bytes=PICK_VMEM),
        cost_estimate=hint(1),
        name="prepare",
    )(me, o_blocks, tokens, q_rows, k_rows, v_rows, o_rows, gains)


def pick(me, choice, candidates):
    used = sorted(set(choice))
    choice = tuple(used.index(n) for n in choice)
    candidates = [candidates[n] for n in used]
    first = candidates[0][0]
    size = sum(value.shape[0] for value in candidates[0])
    values = [value for candidate in candidates for value in candidate]
    return pl.pallas_call(
        functools.partial(pick_kernel, choice, tuple(len(candidate) for candidate in candidates)),
        out_shape=jax.ShapeDtypeStruct((size, *first.shape[1:]), first.dtype),
        in_specs=[SMEM] + [ANY] * len(values),
        out_specs=VMEM,
        scratch_shapes=[pltpu.SemaphoreType.DMA((max(len(candidate) for candidate in candidates),))],
        compiler_params=pltpu.CompilerParams(vmem_limit_bytes=PICK_VMEM),
        cost_estimate=hint(1),
        name="pick",
    )(me, *values)


def body(sizes, tokens, norm_gains, q_blocks, k_blocks, v_blocks, o_blocks, q_rows, k_rows, v_rows, o_rows, mask_blocks):
    sections, fsdp, tensor = sizes
    assert sections == 4 and tensor == 2
    send = lambda value, target: hop(value, sizes, target)
    p = lax.axis_index("pipe")
    z = lax.axis_index("fsdp")
    x = lax.axis_index("tensor")
    per, cols_half, shard, width = q_blocks.shape[1:]
    oper_t, cols_all = o_blocks.shape[1:3]
    cols = cols_half // sections
    rows = tokens.shape[0]
    feats = cols_all * width

    to_x = lambda p, z, x: (p, z, 1 - x)
    to_core = lambda p, z, x: (p ^ 1, z, x)
    to_pipe = lambda d: lambda p, z, x: (p ^ d, z, x)
    me = jnp.stack([p, x]).astype(jnp.int32)
    cut_for = cut(me, q_blocks, k_blocks, v_blocks, o_blocks)
    o_send, piece, packed = prepare(
        after(me, cut_for[2]), o_blocks, tokens, q_rows, k_rows, v_rows, o_rows, norm_gains
    )
    o_came = send(o_send, to_x)
    o_each = o_came.shape[0] // sections
    o_for = [o_came[d * o_each : (d + 1) * o_each] for d in range(sections)]
    packed = jnp.concatenate([packed] + [send(packed, to_pipe(d)) for d in (1, 2, 3)])
    lists = packed[:, : packed.shape[1] - norm_gains.shape[1]]

    pair_up = fsdp == 4
    if pair_up:
        near_z = {0: 1, 3: 2}
        far_z = {0: 2, 3: 1}
        swap_z = {1: 2, 2: 1}
        back_z = {1: 0, 2: 3}
        step = lambda where: (lambda p, z, x: (p, where[z], x) if z in where else None)
        inner = (z == 1) | (z == 2)

    mask = mask_blocks
    if pair_up:
        odd_near = lambda p, z, x: (p, near_z[z], x) if p & 1 and z in near_z else None
        piece = pick(me, (0, 1, 0, 1), [[piece], [send(piece, odd_near)]])
        mask = jnp.where((p & 1) == 1, send(mask, odd_near), mask)

    by_first = lambda p, z, x: (p ^ 2, z, x) if p & 1 else (p, z, 1 - x)
    by_second = lambda p, z, x: (p, z, 1 - x) if p & 1 else (p ^ 2, z, x)

    def share(value):
        first, second = send(value, by_first), send(value, by_second)
        return [value, first, second, send(after(first, second), by_second)]

    def exchange(values, ways):
        return {
            (d, pipes): [send(value, lambda p, z, x: (p ^ d, z, x) if p in pipes else None) for value in values[d]]
            for d, pipes in ways
        }

    def piece_of(section, came):
        keys = list(came)
        choice = []
        for q in range(sections):
            choice.append(next((i for i, (d, pipes) in enumerate(keys) if d == q ^ section and section in pipes), len(keys)))
        return pick(me, tuple(choice), [*came.values(), [cut_for[0], o_for[0]]])

    if pair_up:
        low = z < 2
        pos = jnp.where(low, jnp.array([1, 0, 2, 3]), jnp.array([2, 3, 1, 0])).astype(jnp.int32)

        def first_leg(piece, *tie):
            piece = after(piece, *tie) if tie else piece
            swapped = send(piece, step(swap_z))
            return [piece, send(piece, step(near_z)), swapped]

        def second_leg(leg, *tie):
            return leg + [send(after(leg[0], *leg[1:], *tie), step(far_z))]

        def along_z(piece, tie=()):
            leg = first_leg(piece, *tie)
            return leg + [send(leg[0], step(far_z))]
    else:
        pos = jnp.zeros((1,), jnp.int32)

        def first_leg(piece, *tie):
            return [lax.all_gather(piece, "fsdp", axis=1, tiled=True)]

        def second_leg(leg, *tie):
            return leg

        def along_z(piece, tie=()):
            return [lax.all_gather(piece, "fsdp", axis=1, tiled=True)]

    def with_core(parts):
        return [each for part in parts for each in (part, send(part, to_core))]

    def deliver(core):
        if not pair_up:
            return kept[core]
        return send(
            kept[core],
            lambda p, z, x: (p - (p & 1) + core, back_z[z] if p & 1 else z, x) if z in back_z else None,
        )

    kept = [None, None]
    results = [None, None]
    o_for = [after(value, piece, mask) for value in o_for]
    round_a = exchange(list(zip(cut_for, o_for)), [(2, (0, 3)), (3, (0, 3)), (1, (0, 1, 2, 3))])
    leg = first_leg(piece_of(0, round_a))
    arrived = [value for values in list(round_a.values())[:2] for value in values]
    both_for = {d: [pick(me, (0,) * sections, [[after(cut_for[d], *arrived), o_for[d]]])] for d in (2, 3)}
    u = after(piece, *arrived)
    pieces = share(u)
    both_for = {d: [after(value, *pieces[1:]) for value in values] for d, values in both_for.items()}
    round_b = exchange(both_for, [(2, (1, 2)), (3, (1, 2))])
    round_b[1, (0, 1, 2, 3)] = round_a[1, (0, 1, 2, 3)]
    leg = second_leg(leg, pieces[1], packed)
    coming = None
    most = with_core(leg[:-1])
    in_count = 3 * per * cols
    out_count = leg[0].shape[0] - in_count
    lists_x = send(lists, to_x)
    for s in range(sections):
        last_leg = leg[-1:]
        if s > 0:
            pieces = share(u)
            last_leg = [after(part, pieces[3]) for part in last_leg]
        weights = most + with_core(last_leg)
        if s + 1 < sections:
            coming = piece_of(1, round_b) if s == 0 else coming
            leg = first_leg(coming, *last_leg)
        heads, *before = attend(s, me, lists, packed, pos, mask, pieces, in_count, weights)
        if s > 0:
            core = (s - 1) & 1
            kept[core] = before[0] if kept[core] is None else jnp.where((p >> 1) == 0, kept[core], before[0])
        if s == sections - 1:
            results = [deliver(core) for core in range(2)]
        pieces = share(heads)
        if s + 1 < sections:
            tie = pieces[1:3] if s == 0 else pieces[1:]
            if s + 2 < sections:
                coming = piece_of(s + 2, round_b if s == 0 else round_a)
                tie = [*tie, coming]
            leg = second_leg(leg, *tie)
            most = with_core(leg[:-1])
        if s == sections - 1:
            result = jnp.where((p & 1) == 1, results[1], results[0])
            pieces[0] = after(pieces[0], result)
        u = project_out(s, me, lists, lists_x, 3 * per * cols_half, pos, pieces, u, in_count, out_count, weights)

    final = u
    last_core = (sections - 1) & 1
    if pair_up:
        home = lambda z, core: back_z[z] if core else z
    else:
        home = lambda z, core: z if core == last_core else None
    halves = []
    for y in range(2):

        def to_last(p, z, x, y=y):
            to = home(z, p & 1) if (p >> 1) == y and (not pair_up or z in back_z) else None
            return None if to is None else (sections - 1, to, x)

        halves.append(send(final, to_last))
    made_by = jnp.where(inner, 0, 1) if pair_up else last_core
    blocks = jnp.stack(halves).reshape(2, 2, cols, rows, width)
    blocks = jnp.where(made_by == 1, blocks[:, ::-1], blocks)
    last = jnp.transpose(blocks, (3, 0, 1, 2, 4)).reshape(rows, -1)
    return jnp.where(p == sections - 1, last, result)[None]


def solution(mesh):
    placed = (
        P("fsdp", "tensor"),
        P("pipe", None),
        P("pipe", None, "tensor", "fsdp", None),
        P("pipe", None, "tensor", "fsdp", None),
        P("pipe", None, "tensor", "fsdp", None),
        P("pipe", "tensor", None, "fsdp", None),
        P("pipe", None, "tensor"),
        P("pipe", None, "tensor"),
        P("pipe", None, "tensor"),
        P("pipe", "tensor", None),
        P("fsdp", None, None),
    )
    sizes = tuple(mesh.shape[axis] for axis in AXES)
    return jax.shard_map(
        functools.partial(body, sizes),
        mesh=mesh,
        in_specs=placed,
        out_specs=P("pipe", "fsdp", "tensor"),
        check_vma=False,
    )
```
